512 devices in a mesh: mem: 4 (over z_lo), tile: 128 (over y, z_hi, x, core).
Axes of the slice: x: 4, y: 4, z: 16 (z_hi: 4, z_lo: 4; z = z_hi * 4 + z_lo), core: 2. Of those that a mesh axis runs over, the one named last changes fastest.
Arguments:
- air_fields: bfloat16 [4, 128, 128, 4, 128], P('mem', 'tile'), may hold values from -6 to 6
- sea_warmth: float32 [4, 128, 15, 128], P('mem', 'tile'), may hold values from -6 to 6
- rotation_flags: int32 [128], P('tile'), may hold values from 0 to 1
- sea_pixel_indicator: int32 [128, 4, 128], P('tile'), may hold values 0 or 1
- panel_sea_parcel: int32 [128], replicated, may hold values from 0 to 127, as said below
- opening_filter: bfloat16 [128, 3, 3, 128], replicated, may hold values from -0.1875 to 0.1875
- closing_filter: bfloat16 [128, 3, 3, 128], replicated, may hold values from -0.1875 to 0.1875
- warmth_injection: float32 [128], replicated, may hold values from -4 to 4
- exchange_projection: bfloat16 [16, 128], replicated, may hold values from -0.5 to 0.5
- sea_entry_matrix: float32 [128, 17], replicated, may hold values from -1.5 to 1.5
- sea_exit_matrix: float32 [128], replicated, may hold values from -0.5 to 0.5
- air_adjoint_result: bfloat16 [4, 128, 128, 4, 128], P('mem', 'tile'), may hold values from -6 to 6
- warmth_adjoint_result: float32 [4, 128, 15, 128], P('mem', 'tile'), may hold values from -6 to 6
Outputs:
- next_air_fields: bfloat16 [4, 128, 128, 4, 128], P('mem', 'tile')
- next_sea_warmth: float32 [4, 128, 15, 128], P('mem', 'tile')
- leading_stencil_sensitivity: float32 [128, 3, 3, 128], replicated
- final_stencil_sensitivity: float32 [128, 3, 3, 128], replicated
- heat_inflow_sensitivity: float32 [128], replicated
- coupler_operator_sensitivity: float32 [16, 128], replicated
- grad_ocean_in: float32 [128, 17], replicated
- grad_ocean_out: float32 [128], replicated
The draws below stay inside these ranges and needn't reach their ends.
Inputs may be any that keep to these rules, and one draw needn't show every extreme that they name: `panel_sea_parcel`: the entries of tiles below 120 are a permutation of 0 to 119; every other entry equals its own index. Tile 0's block is held by the last ocean tile, and tile 120 - 1's block by the first. For each ocean tile 120 + j, the tile (120 + j + 64) mod 128, where it is an atmosphere tile other than 0 and 119, has its block held by that ocean tile.
All inputs are finite; a program needn't handle non-finite values. No bound on the sum of `sea_pixel_indicator` on one device may be relied on, other than what follows from the above.
Results may differ from the reference program's by a relative error of at most 0.0082.
Values may be sent and summed in bfloat16 or wider, within the bound.
No kernel may reach another device: no remote copies, remote signals or barrier semaphores. Data moves between devices by JAX's collectives and lax.ppermute only.
A program may use at most 64 MiB of HBM per device.

```python
import math
import jax
import jax.numpy as jnp
from jax import lax

AIR_FEATURES = 128
FX = 16
HO = 128
PANEL_HEIGHT = 4
MESH_WIDTH = 128
PARTICIPANTS = 4
PANEL_COUNT = 128
SEA_PANELS = 8
AIR_PANELS = 120
SEA_PARCELS = 15
LOWRES_PIXELS = 128


def swap_places(order, place, value):
    positions = jnp.arange(AIR_PANELS, dtype=jnp.int32)
    where_value = jnp.sum(jnp.where(order == value, positions, 0)).astype(jnp.int32)
    current = order[place]
    order = jnp.where(positions == where_value, current, order)
    order = jnp.where(positions == place, value, order)
    return order


def avoid_value(value, taken, base_value):
    moved = base_value + (value - base_value + 1) % SEA_PARCELS
    return jnp.where(value == taken, moved, value).astype(jnp.int32)


def draw_panel_sea_parcel(key, part):
    key = jax.random.fold_in(key, 7)
    first_key, last_key, order_key, pair_key = jax.random.split(key, 4)
    order = jax.random.permutation(order_key, AIR_PANELS).astype(jnp.int32)
    late_value = (AIR_PANELS - SEA_PARCELS + jax.random.randint(first_key, (), 0, SEA_PARCELS)).astype(jnp.int32)
    order = swap_places(order, 0, late_value)
    early_value = jax.random.randint(last_key, (), 0, SEA_PARCELS).astype(jnp.int32)
    early_value = jnp.where(early_value == late_value, (early_value + 1) % SEA_PARCELS, early_value).astype(jnp.int32)
    early_value = jnp.where(SEA_PARCELS == AIR_PANELS, order[AIR_PANELS - 1], early_value).astype(jnp.int32)
    order = swap_places(order, AIR_PANELS - 1, early_value)
    for ocean_place in range(SEA_PANELS):
        partner = (AIR_PANELS + ocean_place + PANEL_COUNT // 2) % PANEL_COUNT
        if partner < AIR_PANELS and partner != 0 and (partner != AIR_PANELS - 1):
            base_value = ocean_place * SEA_PARCELS
            pick = (base_value + jax.random.randint(jax.random.fold_in(pair_key, ocean_place), (), 0, SEA_PARCELS)).astype(jnp.int32)
            pick = avoid_value(pick, late_value, base_value)
            pick = avoid_value(pick, early_value, base_value)
            pick = avoid_value(pick, late_value, base_value)
            order = swap_places(order, partner, pick)
    return jnp.concatenate([order, jnp.arange(AIR_PANELS, PANEL_COUNT, dtype=jnp.int32)])


def plant(drawn, key, least, top_value):
    shape = drawn.shape
    index_at = [jax.random.randint(jax.random.fold_in(key, axis), (), 0, shape[axis]) for axis in range(len(shape))]
    drawn = drawn.at[tuple(index_at)].set(least)
    longest = shape.index(max(shape))
    index_at[longest] = (index_at[longest] + 1) % shape[longest]
    return drawn.at[tuple(index_at)].set(top_value)


def levels(rng, dims, cuts, smallest, high):
    factor_of, own = 1.0, jax.random.fold_in(rng, 6)
    for axis_at, shards_of in cuts:
        steps = jnp.exp(jax.random.uniform(jax.random.fold_in(own, axis_at), (shards_of,), jnp.float32, smallest / len(cuts), high / len(cuts)))
        factor_of = factor_of * jnp.repeat(steps, dims[axis_at] // shards_of).reshape([-1 if axis == axis_at else 1 for axis in range(len(dims))])
    return factor_of


def bell_draw(key, extent, spread, most, cuts=(), kind=jnp.bfloat16):
    drawn = jax.random.normal(key, extent, jnp.float32) * spread
    if len(cuts) > 0:
        drawn = levels(key, extent, cuts, -0.22, 0.18) * drawn
    return jnp.clip(drawn, min=-most, max=most).astype(kind)


def setup_inputs(seed: int = 0) -> dict:
    seeds = jax.random.split(jax.random.key(seed), 14)
    return {
        "air_fields": bell_draw(seeds[0], (PARTICIPANTS, PANEL_COUNT, AIR_FEATURES, PANEL_HEIGHT, MESH_WIDTH), 1.0, 6.0, ((0, 4), (1, 128))),
        "sea_warmth": bell_draw(seeds[1], (PARTICIPANTS, PANEL_COUNT, SEA_PARCELS, LOWRES_PIXELS), 1.0, 6.0, ((0, 4), (1, 128)), jnp.float32),
        "rotation_flags": plant(jax.random.randint(seeds[2], (PANEL_COUNT,), 0, 2), jax.random.fold_in(seeds[2], 1), 0, 1).astype(jnp.int32),
        "sea_pixel_indicator": plant((jax.random.randint(seeds[3], (PANEL_COUNT, PANEL_HEIGHT, MESH_WIDTH), 0, 3) < 2).astype(jnp.int32), jax.random.fold_in(seeds[3], 1), 0, 1),
        "panel_sea_parcel": draw_panel_sea_parcel(jax.random.fold_in(seeds[13], 71), 0),
        "opening_filter": bell_draw(seeds[5], (AIR_FEATURES, 3, 3, AIR_FEATURES), (9 * AIR_FEATURES) ** -0.5, 0.1875),
        "closing_filter": bell_draw(seeds[6], (AIR_FEATURES, 3, 3, AIR_FEATURES), (9 * AIR_FEATURES) ** -0.5, 0.1875),
        "warmth_injection": bell_draw(seeds[7], (AIR_FEATURES,), 1.0, 4.0, (), jnp.float32),
        "exchange_projection": bell_draw(seeds[8], (FX, AIR_FEATURES), AIR_FEATURES ** -0.5, 0.5),
        "sea_entry_matrix": bell_draw(seeds[9], (HO, FX + 1), (FX + 1) ** -0.5, 1.5, (), jnp.float32),
        "sea_exit_matrix": bell_draw(seeds[10], (HO,), HO ** -0.5, 0.5, (), jnp.float32),
        "air_adjoint_result": bell_draw(seeds[11], (PARTICIPANTS, PANEL_COUNT, AIR_FEATURES, PANEL_HEIGHT, MESH_WIDTH), 1.0, 6.0, ((0, 4), (1, 128))),
        "warmth_adjoint_result": bell_draw(seeds[12], (PARTICIPANTS, PANEL_COUNT, SEA_PARCELS, LOWRES_PIXELS), 1.0, 6.0, ((0, 4), (1, 128)), jnp.float32),
    }


gelu_scale = math.sqrt(2.0 / math.pi)
gelu_cubic = 0.044715

def gelu_pair(value):
    inner = gelu_scale * (value + gelu_cubic * value * value * value)
    tanh_val = jnp.tanh(inner)
    out = 0.5 * value * (1.0 + tanh_val)
    slope = 0.5 * (1.0 + tanh_val) + 0.5 * value * (1.0 - tanh_val * tanh_val) * gelu_scale * (1.0 + 3.0 * gelu_cubic * value * value)
    return (out, slope)

def coarsen(value):
    new_shape = value.shape[:-2] + (value.shape[-2] // 2, 2, value.shape[-1] // 2, 2)
    return value.reshape(new_shape).sum(axis=(-3, -1))

def highres_pixels(value):
    return jnp.repeat(jnp.repeat(value, 2, axis=-2), 2, axis=-1)

def patches(padded, row_count):
    pieces = [jnp.roll(padded[:, row_step:row_step + row_count], 1 - col_step, axis=2) for row_step in range(3) for col_step in range(3)]
    return jnp.concatenate(pieces, axis=0)

def back_patches(padded, row_count):
    pieces = [jnp.roll(padded[:, 2 - row_step:2 - row_step + row_count], col_step - 1, axis=2) for row_step in range(3) for col_step in range(3)]
    return jnp.concatenate(pieces, axis=0)

def apply_kernel(kernel_flat, patch):
    outputs = jnp.dot(kernel_flat, patch.reshape(patch.shape[0], -1), preferred_element_type=jnp.float32)
    return outputs.reshape((kernel_flat.shape[0],) + patch.shape[1:])

def kernel_grad(cot_b, patch):
    return lax.dot_general(cot_b.reshape(cot_b.shape[0], -1), patch.reshape(patch.shape[0], -1), (((1,), (1,)), ((), ())), preferred_element_type=jnp.float32)

def sea_increment(warmth_lines, exchange_line_amounts, adjoint_lines, sea_entry_matrix, sea_exit_matrix):
    exact_arithmetic_option = lax.Precision.HIGHEST
    before_nonlinearity = sea_entry_matrix[:, 0][None, :, None] * warmth_lines[:, None, :] + jnp.einsum('bw,pwx->pbx', sea_entry_matrix[:, 1:], exchange_line_amounts, precision=exact_arithmetic_option)
    latent_features, slope = gelu_pair(before_nonlinearity)
    next_lines = warmth_lines + jnp.einsum('o,los->ls', sea_exit_matrix, latent_features, precision=exact_arithmetic_option)
    outflow_operator_sensitivity = jnp.einsum('lc,lhc->h', adjoint_lines, latent_features, precision=exact_arithmetic_option)
    before_nonlinearity_adjoint = sea_exit_matrix[None, :, None] * adjoint_lines[:, None, :] * slope
    warmth_derivative = jnp.einsum('ajh,ah->j', before_nonlinearity_adjoint, warmth_lines, precision=exact_arithmetic_option)
    coupler_operator_sensitivity = jnp.einsum('lhc,lfc->hf', before_nonlinearity_adjoint, exchange_line_amounts, precision=exact_arithmetic_option)
    inflow_operator_sensitivity = jnp.concatenate([warmth_derivative[:, None], coupler_operator_sensitivity], axis=1)
    exchange_adjoint_amount = jnp.einsum('hf,lhc->lfc', sea_entry_matrix[:, 1:], before_nonlinearity_adjoint, precision=exact_arithmetic_option)
    return (next_lines, exchange_adjoint_amount, inflow_operator_sensitivity, outflow_operator_sensitivity)

def reference(air_fields, sea_warmth, rotation_flags, sea_pixel_indicator, panel_sea_parcel, opening_filter, closing_filter, warmth_injection, exchange_projection, sea_entry_matrix, sea_exit_matrix, air_adjoint_result, warmth_adjoint_result):
    exact_arithmetic_option = lax.Precision.HIGHEST
    parcel_offsets = panel_sea_parcel[:AIR_PANELS].astype(jnp.int32)
    flipped = (rotation_flags[:AIR_PANELS] == 1)[:, None, None, None]
    repeated_indicator = sea_pixel_indicator[:AIR_PANELS].astype(jnp.float32)
    inv_count = 1.0 / jnp.maximum(coarsen(repeated_indicator), 1.0)
    rows_all = AIR_PANELS * PANEL_HEIGHT
    first_flat = opening_filter.reshape(AIR_FEATURES, 9 * AIR_FEATURES)
    second_flat = closing_filter.reshape(AIR_FEATURES, 9 * AIR_FEATURES)
    first_back = jnp.transpose(opening_filter, (3, 1, 2, 0)).reshape(AIR_FEATURES, 9 * AIR_FEATURES)
    second_back = jnp.transpose(closing_filter, (3, 1, 2, 0)).reshape(AIR_FEATURES, 9 * AIR_FEATURES)

    def orient_tiles(value):
        return jnp.where(flipped, value[..., ::-1, ::-1], value)

    def to_grid(value):
        return jnp.transpose(value, (1, 0, 2, 3)).reshape(value.shape[1], rows_all, MESH_WIDTH)

    def from_grid(value):
        return jnp.transpose(value.reshape(value.shape[0], AIR_PANELS, PANEL_HEIGHT, MESH_WIDTH), (1, 0, 2, 3))

    def pad_rows(value):
        return jnp.pad(value, ((0, 0), (1, 1), (0, 0)))

    def single_participant_advance(participant_number):
        participant_air, participant_warmth, participant_air_adjoint, participant_warmth_adjoint = participant_number
        warmth_parcels = participant_warmth[AIR_PANELS:].reshape(AIR_PANELS, LOWRES_PIXELS)
        panel_warmth = warmth_parcels[parcel_offsets]
        boundary_panel_amounts = highres_pixels(panel_warmth.reshape(AIR_PANELS, PANEL_HEIGHT // 2, MESH_WIDTH // 2)) * repeated_indicator
        border_quantities = boundary_panel_amounts.reshape(rows_all, MESH_WIDTH)
        starting_mesh = to_grid(orient_tiles(participant_air[:AIR_PANELS]))
        combined_source = (starting_mesh.astype(jnp.float32) + warmth_injection[:, None, None] * border_quantities[None]).astype(jnp.bfloat16)
        in_patch = patches(pad_rows(combined_source), rows_all)
        pre_first = apply_kernel(first_flat, in_patch)
        act_out, slope = gelu_pair(pre_first)
        act_b = act_out.astype(jnp.bfloat16)
        act_patch = patches(pad_rows(act_b), rows_all)
        state_new = combined_source.astype(jnp.float32) + apply_kernel(second_flat, act_patch)
        state_b = state_new.astype(jnp.bfloat16)
        new_tiles = orient_tiles(from_grid(state_b))
        worker_later_climate = jnp.concatenate([new_tiles, jnp.zeros((SEA_PANELS, AIR_FEATURES, PANEL_HEIGHT, MESH_WIDTH), jnp.bfloat16)], axis=0)
        flux_raw = jnp.dot(exchange_projection, state_b.reshape(AIR_FEATURES, -1), preferred_element_type=jnp.float32).reshape(FX, rows_all, MESH_WIDTH)
        flux_tiles = from_grid(flux_raw)
        flux_b = (coarsen(flux_tiles * repeated_indicator[:, None]) * inv_count[:, None]).reshape(AIR_PANELS, FX, LOWRES_PIXELS).astype(jnp.bfloat16)
        exchange_by_parcel = jnp.zeros((AIR_PANELS, FX, LOWRES_PIXELS), jnp.bfloat16).at[parcel_offsets].set(flux_b)
        adjoint_parcels = participant_warmth_adjoint[AIR_PANELS:].reshape(AIR_PANELS, LOWRES_PIXELS)
        next_lines, exchange_adjoint_amount, inflow_operator_sensitivity, outflow_operator_sensitivity = sea_increment(warmth_parcels, exchange_by_parcel.astype(jnp.float32), adjoint_parcels, sea_entry_matrix, sea_exit_matrix)
        worker_later_heat = jnp.concatenate([jnp.zeros((AIR_PANELS, SEA_PARCELS, LOWRES_PIXELS), jnp.float32), next_lines.reshape(SEA_PANELS, SEA_PARCELS, LOWRES_PIXELS)], axis=0)
        tile_cot = exchange_adjoint_amount[parcel_offsets].reshape(AIR_PANELS, FX, PANEL_HEIGHT // 2, MESH_WIDTH // 2) * inv_count[:, None]
        fine_tiles = highres_pixels(tile_cot) * repeated_indicator[:, None]
        fine_cot = to_grid(fine_tiles).reshape(FX, -1)
        coupler_operator_sensitivity = lax.dot_general(fine_cot, state_b.astype(jnp.float32).reshape(AIR_FEATURES, -1), (((1,), (1,)), ((), ())), precision=exact_arithmetic_option)
        out_cot = to_grid(orient_tiles(participant_air_adjoint[:AIR_PANELS])).astype(jnp.float32)
        back_flux = lax.dot_general(exchange_projection.astype(jnp.float32), fine_cot, (((0,), (0,)), ((), ())), precision=exact_arithmetic_option)
        state_cot = out_cot + back_flux.reshape(AIR_FEATURES, rows_all, MESH_WIDTH)
        state_cot_b = state_cot.astype(jnp.bfloat16)
        final_stencil_sensitivity = kernel_grad(state_cot_b, act_patch).reshape(AIR_FEATURES, 3, 3, AIR_FEATURES)
        act_cot = apply_kernel(second_back, back_patches(pad_rows(state_cot_b), rows_all))
        pre_cot_b = (act_cot * slope).astype(jnp.bfloat16)
        leading_stencil_sensitivity = kernel_grad(pre_cot_b, in_patch).reshape(AIR_FEATURES, 3, 3, AIR_FEATURES)
        arriving_sensitivity = state_cot + apply_kernel(first_back, back_patches(pad_rows(pre_cot_b), rows_all))
        heat_inflow_sensitivity = lax.optimization_barrier(jnp.sum(arriving_sensitivity * border_quantities[None], axis=(1, 2)))
        return (worker_later_climate, worker_later_heat, (leading_stencil_sensitivity, final_stencil_sensitivity, heat_inflow_sensitivity, coupler_operator_sensitivity, inflow_operator_sensitivity, outflow_operator_sensitivity))
    next_air_fields, next_sea_warmth, derivative_collection = lax.map(single_participant_advance, (air_fields, sea_warmth, air_adjoint_result, warmth_adjoint_result))
    norm_scale = 1.0 / math.sqrt(PARTICIPANTS * AIR_PANELS * PANEL_HEIGHT * MESH_WIDTH)
    running_totals = [lax.optimization_barrier(jnp.sum(item, axis=0)) * norm_scale for item in derivative_collection]
    return (next_air_fields, next_sea_warmth, running_totals[0], running_totals[1], running_totals[2], running_totals[3], running_totals[4], running_totals[5])
```

```python
import math

import jax
import jax.numpy as jnp
from jax import lax
from jax.experimental import pallas as pl
from jax.experimental.pallas import tpu as pltpu
from jax.sharding import Mesh, PartitionSpec as P

CH = 128
FX = 16
ROWS = 4
TILES = 128
AIR = 120
LINES = 15
CHUNK = 80
PAY = 32 * CHUNK
HALO = 6 * CH + 16
TILE_AXES = ("y", "zh", "x", "core")
PLANE = ("y", "x", "core")

gelu_scale = math.sqrt(2.0 / math.pi)
gelu_cubic = 0.044715
norm_scale = 1.0 / math.sqrt(4 * AIR * ROWS * CH)
EXACT = lax.Precision.HIGHEST
f32 = jnp.float32
bf16 = jnp.bfloat16


def gelu_pair(value):
    square = value * value
    inner = gelu_scale * (value + gelu_cubic * square * value)
    tanh_val = jnp.tanh(inner)
    out = 0.5 * value * (1.0 + tanh_val)
    slope = 0.5 * (1.0 + tanh_val) + 0.5 * value * (1.0 - tanh_val * tanh_val) * gelu_scale * (
        1.0 + 3.0 * gelu_cubic * square
    )
    return (out, slope)


def dot(a, b, precision=None):
    return lax.dot_general(
        a, b, (((1,), (0,)), ((), ())), precision=precision, preferred_element_type=f32
    )


def dot_nt(a, b, precision=None):
    return lax.dot_general(
        a, b, (((1,), (1,)), ((), ())), precision=precision, preferred_element_type=f32
    )


def blk(i, n=1):
    return slice(i * CH, (i + n) * CH)


def step_kernel(
    ok_ref,
    warm_ref,
    below_ref,
    own_ref,
    adj_ref,
    above_ref,
    k1_ref,
    k2_ref,
    k1b_ref,
    k2b_ref,
    cols_ref,
    proj_ref,
    projt_ref,
    entry_ref,
    entryt_ref,
    next_ref,
    pay_ref,
    mixed_roll,
    act_roll,
    cot_roll,
    pre_roll,
    slope_ref,
    small_ref,
):
    ok = (ok_ref[0], ok_ref[1], ok_ref[2])
    winj, entry0, exit_col = cols_ref[:, 0:1], cols_ref[:, 1:2], cols_ref[:, 2:3]

    def put_rolled(ref, i, value, back=False):
        ref[blk(0), blk(i)] = pltpu.roll(value, CH - 1 if back else 1, 1).astype(bf16)
        ref[blk(1), blk(i)] = value.astype(bf16)
        ref[blk(2), blk(i)] = pltpu.roll(value, 1 if back else CH - 1, 1).astype(bf16)

    sea_rows = []
    for ref, at in ((below_ref, 6 * CH), (own_ref, 4 * CH), (above_ref, 6 * CH)):
        ind = ref[at : at + 16, :].astype(f32)
        sea_rows += [ind[r : r + 1] for r in range(ROWS)]
    cell = lax.broadcasted_iota(jnp.int32, (CH, 2 * CH), 1)
    entry_at = lax.broadcasted_iota(jnp.int32, (CH, 2 * CH), 0)
    spread = (entry_at == (cell // CH) * 64 + (cell % CH) // 2).astype(f32)
    on_cells = dot(warm_ref[...], spread, EXACT)
    warm = [[on_cells[i : i + 1, blk(r)] * ok[i] for r in range(2)] for i in range(3)]
    warm_adj = [[on_cells[3 + i : 4 + i, blk(r)] * ok[i] for r in range(2)] for i in range(3)]
    surface = [warm[r // 4][(r % 4) // 2] * sea_rows[r] for r in range(12)]

    for r in range(12):
        ref = (below_ref, own_ref, above_ref)[r // 4]
        value = ref[blk(r % 4), :].astype(f32) * ok[r // 4] + winj * surface[r]
        put_rolled(mixed_roll, r, value.astype(bf16).astype(f32))

    pre_first = dot(k1_ref[:, 0:384], mixed_roll[:, blk(0, 10)])
    pre_first += dot(k1_ref[:, 384:768], mixed_roll[:, blk(1, 10)])
    pre_first += dot(k1_ref[:, 768:1152], mixed_roll[:, blk(2, 10)])
    for i in range(10):
        act, slope = gelu_pair(pre_first[:, blk(i)])
        m = ok[(i + 1) // 4]
        put_rolled(act_roll, i, (act * m).astype(bf16).astype(f32))
        if 2 <= i < 8:
            slope_ref[:, blk(i - 2)] = slope * m

    state = dot(k2_ref[:, 0:384], act_roll[:, blk(0, 8)])
    state += dot(k2_ref[:, 384:768], act_roll[:, blk(1, 8)])
    state += dot(k2_ref[:, 768:1152], act_roll[:, blk(2, 8)])
    state_rows = []
    for i in range(8):
        row = (state[:, blk(i)] + mixed_roll[blk(1), blk(i + 2)].astype(f32)) * ok[(i + 2) // 4]
        state_rows.append(row.astype(bf16))
    state_b = jnp.concatenate(state_rows, axis=1)
    for r in range(ROWS):
        next_ref[blk(r), :] = state_rows[2 + r]

    flux = dot(proj_ref[...], state_b)
    even = lax.broadcasted_iota(jnp.int32, (FX, CH), 1) % 2 == 0

    def pair_sum(v):
        return v + jnp.where(even[: v.shape[0]], pltpu.roll(v, CH - 1, 1), pltpu.roll(v, 1, 1))

    tile_flux, inv_count = [], []
    for q in range(4):
        sea_a, sea_b = sea_rows[2 + 2 * q], sea_rows[3 + 2 * q]
        count = pair_sum(jnp.broadcast_to(sea_a + sea_b, (FX, CH)))
        inv = 1.0 / jnp.maximum(count, 1.0)
        total = pair_sum(flux[:, blk(2 * q)] * sea_a + flux[:, blk(2 * q + 1)] * sea_b)
        tile_flux.append((total * inv).astype(bf16).astype(f32))
        inv_count.append(inv)
    block_flux = jnp.concatenate(tile_flux, axis=1)
    block_warm = jnp.concatenate([warm[0][1], warm[1][0], warm[1][1], warm[2][0]], axis=1)
    block_adj = jnp.concatenate(
        [warm_adj[0][1], warm_adj[1][0], warm_adj[1][1], warm_adj[2][0]], axis=1
    )

    pre_ocean = entry0 * block_warm + dot(entry_ref[...], block_flux, EXACT)
    latent, ocean_slope = gelu_pair(pre_ocean)
    ocean_cot = exit_col * block_adj * ocean_slope
    flux_cot = dot(entryt_ref[...], ocean_cot, EXACT)
    increment = jnp.sum(exit_col * latent[:, blk(1, 2)], axis=0, keepdims=True)
    increment = 0.5 * dot_nt(jnp.broadcast_to(increment, (16, 2 * CH)), spread, EXACT)
    small_ref[16:32, :] = 0.5 * dot_nt(block_flux[:, blk(1, 2)], ocean_cot[:, blk(1, 2)], EXACT)
    own_warm = jnp.broadcast_to(block_warm[:, blk(1, 2)], (8, 2 * CH))
    own_adj = jnp.broadcast_to(block_adj[:, blk(1, 2)], (8, 2 * CH))
    grad_warm = 0.5 * dot_nt(own_warm, ocean_cot[:, blk(1, 2)], EXACT)
    grad_out = 0.5 * dot_nt(own_adj, latent[:, blk(1, 2)], EXACT)

    fine_cot = jnp.concatenate(
        [flux_cot[:, blk(i // 2)] * inv_count[i // 2] * sea_rows[2 + i] for i in range(8)], axis=1
    )
    small_ref[0:16, :] = dot_nt(fine_cot[:, blk(2, 4)], state_b[:, blk(2, 4)].astype(f32), EXACT)
    back_flux = dot(projt_ref[...], fine_cot, EXACT)
    own_cot = []
    for i in range(8):
        if i < 2:
            out_cot = below_ref[blk(4 + i), :]
        elif i < 6:
            out_cot = adj_ref[blk(i - 2), :]
        else:
            out_cot = above_ref[blk(4 + i - 6), :]
        row = (out_cot.astype(f32) + back_flux[:, blk(i)]) * ok[(i + 2) // 4]
        put_rolled(cot_roll, i, row.astype(bf16).astype(f32), True)
        if 2 <= i < 6:
            own_cot.append(row)

    def put_slab(s, value):
        if s < 15:
            pay_ref[blk(s), :] = value.astype(bf16)
        else:
            at = 24 * CHUNK + 2 * (s - 15) * CHUNK
            pay_ref[at : at + 64, :] = value[0:64].astype(bf16)
            pay_ref[at + CHUNK : at + CHUNK + 64, :] = value[64:128].astype(bf16)

    cot_own = cot_roll[blk(1), blk(2, 4)]
    for a in range(3):
        grad = dot_nt(cot_own, act_roll[:, blk(a + 2, 4)])
        for b in range(3):
            put_slab(9 + 3 * a + b, grad[:, blk(b)])

    act_cot = dot(k2b_ref[:, 0:384], cot_roll[:, blk(2, 6)])
    act_cot += dot(k2b_ref[:, 384:768], cot_roll[:, blk(1, 6)])
    act_cot += dot(k2b_ref[:, 768:1152], cot_roll[:, blk(0, 6)])
    for i in range(6):
        row = act_cot[:, blk(i)] * slope_ref[:, blk(i)]
        put_rolled(pre_roll, i, row.astype(bf16).astype(f32), True)

    pre_own = pre_roll[blk(1), blk(1, 4)]
    for a in range(3):
        grad = dot_nt(pre_own, mixed_roll[:, blk(a + 3, 4)])
        for b in range(3):
            put_slab(3 * a + b, grad[:, blk(b)])

    in_cot = jnp.concatenate(own_cot, axis=1)
    in_cot += dot(k1b_ref[:, 0:384], pre_roll[:, blk(2, 4)])
    in_cot += dot(k1b_ref[:, 384:768], pre_roll[:, blk(1, 4)])
    in_cot += dot(k1b_ref[:, 768:1152], pre_roll[:, blk(0, 4)])
    own_surface = jnp.broadcast_to(jnp.concatenate(surface[4:8], axis=1), (8, 4 * CH))
    grad_heat = dot_nt(own_surface, in_cot, EXACT)
    row_at = lax.broadcasted_iota(jnp.int32, (16, CH), 0)
    tail = jnp.where(row_at == 0, grad_warm[0:1], 0.0)
    tail = jnp.where(row_at == 1, grad_out[0:1], tail)
    small_ref[32:48, :] = jnp.where(row_at == 2, grad_heat[0:1], tail)

    at = 30 * CHUNK
    pay_ref[at : at + 48, :] = small_ref[...].astype(bf16)
    pay_ref[at + 48 : at + 64, :] = jnp.zeros((16, CH), bf16)
    pay_ref[at + CHUNK : at + CHUNK + 64, :] = jnp.zeros((64, CH), bf16)
    for k in range(8):
        at = (24 + k) * CHUNK + 64
        pay_ref[at : at + 16, :] = increment.astype(bf16)


def run_step(*args):
    vmem = pl.BlockSpec(memory_space=pltpu.VMEM)
    return pl.pallas_call(
        step_kernel,
        out_shape=(
            jax.ShapeDtypeStruct((ROWS * CH, CH), bf16),
            jax.ShapeDtypeStruct((PAY, CH), bf16),
        ),
        in_specs=[pl.BlockSpec(memory_space=pltpu.SMEM)] + [vmem] * (len(args) - 1),
        out_specs=(vmem, vmem),
        scratch_shapes=[
            pltpu.VMEM((3 * CH, 12 * CH), bf16),
            pltpu.VMEM((3 * CH, 10 * CH), bf16),
            pltpu.VMEM((3 * CH, 8 * CH), bf16),
            pltpu.VMEM((3 * CH, 6 * CH), bf16),
            pltpu.VMEM((CH, 6 * CH), f32),
            pltpu.VMEM((48, CH), f32),
        ],
        compiler_params=pltpu.CompilerParams(vmem_limit_bytes=40 * 1024 * 1024),
        cost_estimate=pl.CostEstimate(
            flops=1_500_000_000, bytes_accessed=4_000_000, transcendentals=300_000
        ),
    )(*args)


def exchange(value, axes):
    return lax.all_to_all(value, axes, 0, 0, tiled=True)


def local(
    air_fields,
    sea_warmth,
    rotation_flags,
    sea_pixel_indicator,
    panel_sea_parcel,
    opening_filter,
    closing_filter,
    warmth_injection,
    exchange_projection,
    sea_entry_matrix,
    sea_exit_matrix,
    air_adjoint_result,
    warmth_adjoint_result,
):
    place = lax.axis_index(TILE_AXES)
    in_row = lax.axis_index(("x", "core"))
    flipped = rotation_flags[0] == 1

    held = jnp.pad(
        jnp.stack([sea_warmth[0, 0], warmth_adjoint_result[0, 0]]), ((0, 0), (0, 1), (0, 0))
    ).reshape(32, CH)
    table = exchange(jnp.broadcast_to(held[None], (8, 32, CH)), ("x", "core")).reshape(256, CH)
    padded = jnp.pad(panel_sea_parcel, (1, 8))
    wanted = []
    for field in range(2):
        for step in range(3):
            slot = lax.dynamic_slice(padded, (in_row + step,), (128,))[::8]
            wanted.append((slot // LINES) * 32 + field * 16 + slot % LINES)
    wanted += [jnp.full((16,), -1, jnp.int32)] * 2
    wanted = jnp.stack(wanted, axis=1).reshape(128, 1)
    chooser = (wanted == jnp.arange(256, dtype=jnp.int32)[None]).astype(f32)
    leaving = jnp.dot(chooser, table, precision=EXACT).reshape(16, 8, CH)
    warm = exchange(leaving, ("y", "zh"))[15]

    def canonical(value):
        value = jnp.where(flipped, value[:, ::-1, ::-1], value)
        return jnp.transpose(value, (1, 0, 2)).reshape(ROWS * CH, CH)

    start = canonical(air_fields[0, 0])
    adjoint = canonical(air_adjoint_result[0, 0])
    sea = jnp.pad(sea_pixel_indicator[0].astype(bf16), ((0, 12), (0, 0)))
    up = [(i, i + 1) for i in range(TILES - 1)]
    down = [(i + 1, i) for i in range(TILES - 1)]
    below = lax.ppermute(jnp.concatenate([start, adjoint[2 * CH :], sea]), TILE_AXES, up)
    above = lax.ppermute(jnp.concatenate([start, adjoint[: 2 * CH], sea]), TILE_AXES, down)
    own = jnp.concatenate([start, sea])

    flags = jnp.stack([place > 0, place >= 0, place < AIR - 1, place < 0])
    ok = (flags & (place < AIR)).astype(f32)
    cols = jnp.stack(
        [warmth_injection, sea_entry_matrix[:, 0], sea_exit_matrix, sea_exit_matrix], axis=1
    )
    flat = (CH, 9 * CH)
    next_rows, pay = run_step(
        ok,
        warm,
        below,
        own,
        adjoint,
        above,
        opening_filter.reshape(flat),
        closing_filter.reshape(flat),
        jnp.transpose(opening_filter, (3, 1, 2, 0)).reshape(flat),
        jnp.transpose(closing_filter, (3, 1, 2, 0)).reshape(flat),
        cols,
        exchange_projection,
        exchange_projection.T.astype(f32),
        sea_entry_matrix[:, 1:],
        sea_entry_matrix[:, 1:].T,
    )

    parts = exchange(pay.reshape(32, CHUNK, CH), PLANE)
    partial = jnp.sum(parts.astype(f32), axis=0)
    y, zh, x, core = (lax.axis_index(a) for a in TILE_AXES)
    slots = lax.dynamic_index_in_dim(panel_sea_parcel.reshape(4, 4, 8), zh, 1, keepdims=False)
    slots = slots.reshape(1, 32)
    source = jnp.arange(4)[:, None] * 32 + zh * 8 + jnp.arange(8)[None]
    mine = (slots // LINES == in_row) & (source.reshape(1, 32) < AIR)
    line_at = jnp.arange(16, dtype=jnp.int32)[:, None]
    place_line = (mine & (slots % LINES == line_at)).astype(bf16)
    lines = jnp.dot(place_line, parts[:, 64], preferred_element_type=f32)
    column = jnp.concatenate([partial, lines]).astype(bf16)
    column = exchange(jnp.broadcast_to(column[None], (16, CHUNK + 16, CH)), ("zh", "mem"))
    total = jnp.sum(column[:, :CHUNK].astype(f32), axis=0) * norm_scale
    lines = lax.dynamic_index_in_dim(
        column[:, CHUNK : CHUNK + LINES].reshape(4, 4, LINES, CH),
        lax.axis_index("mem"),
        1,
        keepdims=False,
    )
    next_sea = sea_warmth[0, 0] + jnp.sum(lines.astype(f32), axis=0)
    next_sea = jnp.where(place < AIR, 0.0, next_sea)
    whole = exchange(jnp.broadcast_to(total.astype(bf16)[None], (32, CHUNK, CH)), PLANE)
    tail = whole[24:, :64].reshape(512, CH)
    slabs = jnp.concatenate([whole[:24].reshape(24 * CHUNK, CH), tail[: 3 * CH]])
    slabs = jnp.transpose(slabs.reshape(2, 3, 3, CH, CH), (0, 3, 1, 2, 4)).astype(f32)
    small = tail[3 * CH : 3 * CH + 48].astype(f32)

    next_air = jnp.transpose(next_rows.reshape(ROWS, CH, CH), (1, 0, 2))
    next_air = jnp.where(flipped, next_air[:, ::-1, ::-1], next_air)
    return (
        next_air[None, None],
        next_sea[None, None],
        slabs[0],
        slabs[1],
        small[34],
        small[0:16],
        jnp.concatenate([small[32:33], small[16:32]]).T,
        small[33],
    )


def solution(mesh):
    fine = Mesh(mesh.devices.reshape(4, 4, 4, 4, 2), ("mem",) + TILE_AXES)
    tiles = P("mem", TILE_AXES)
    return jax.shard_map(
        local,
        mesh=fine,
        in_specs=(tiles, tiles, P(TILE_AXES), P(TILE_AXES))
        + (P(),) * 7
        + (tiles, tiles),
        out_specs=(tiles, tiles) + (P(),) * 6,
        check_vma=False,
    )
```

```python
import math

import jax
import jax.numpy as jnp
from jax import lax
from jax.experimental import pallas as pl
from jax.experimental.pallas import tpu as pltpu
from jax.sharding import Mesh, PartitionSpec as P

CH = 128
FX = 16
ROWS = 4
TILES = 128
AIR = 120
LINES = 15
CHUNK = 80
PAY = 32 * CHUNK
HALO = 6 * CH + 16
TILE_AXES = ("y", "zh", "x", "core")
PLANE = ("y", "x", "core")

gelu_scale = math.sqrt(2.0 / math.pi)
gelu_cubic = 0.044715
norm_scale = 1.0 / math.sqrt(4 * AIR * ROWS * CH)
EXACT = lax.Precision.HIGHEST
f32 = jnp.float32
SMALL = pltpu.CompilerParams(vmem_limit_bytes=12 * 1024 * 1024)
bf16 = jnp.bfloat16


def gelu_pair(value):
    square = value * value
    inner = gelu_scale * (value + gelu_cubic * square * value)
    tanh_val = jnp.tanh(inner)
    out = 0.5 * value * (1.0 + tanh_val)
    slope = 0.5 * (1.0 + tanh_val) + 0.5 * value * (1.0 - tanh_val * tanh_val) * gelu_scale * (
        1.0 + 3.0 * gelu_cubic * square
    )
    return (out, slope)


def dot(a, b, precision=None):
    return lax.dot_general(
        a, b, (((1,), (0,)), ((), ())), precision=precision, preferred_element_type=f32
    )


def dot_nt(a, b, precision=None):
    return lax.dot_general(
        a, b, (((1,), (1,)), ((), ())), precision=precision, preferred_element_type=f32
    )


def blk(i, n=1):
    return slice(i * CH, (i + n) * CH)


def tile_place():
    y, zh, x, core = (lax.axis_index(a) for a in TILE_AXES)
    return ((y * 4 + zh) * 4 + x) * 2 + core


def step_kernel(
    warm_ref,
    from_near_ref,
    near_ref,
    far_ref,
    from_far_ref,
    k1_ref,
    k2_ref,
    k1b_ref,
    k2b_ref,
    winj_ref,
    exit_ref,
    proj_ref,
    entry_ref,
    next_ref,
    pay_ref,
    mixed_roll,
    act_roll,
    cot_roll,
    pre_roll,
    slope_ref,
    small_ref,
    ocean_in_ref,
    entry_pad_ref,
):
    place = tile_place()
    mid = place < AIR
    ok = [jnp.where(t, 1.0, 0.0) for t in ((place > 0) & mid, mid, place < AIR - 1)]
    even = lax.axis_index("core") == 0
    cols = jnp.concatenate([winj_ref[...], exit_ref[...], jnp.zeros((6, CH), f32)], axis=0).T
    winj, exit_col = cols[:, 0:1], cols[:, 1:2]

    def below(at):
        return jnp.where(even, from_far_ref[at, :].astype(f32), from_near_ref[at, :].astype(f32))

    def above(at):
        return jnp.where(even, from_near_ref[at, :].astype(f32), from_far_ref[at, :].astype(f32))

    def own(at):
        return near_ref[at, :].astype(f32)

    def taps(ref, a):
        return jnp.concatenate([ref[blk(3 * a + b), :] for b in range(3)], axis=1)

    def put_rolled(ref, i, value, back=False):
        ref[blk(0), blk(i)] = pltpu.roll(value, CH - 1 if back else 1, 1).astype(bf16)
        ref[blk(1), blk(i)] = value.astype(bf16)
        ref[blk(2), blk(i)] = pltpu.roll(value, 1 if back else CH - 1, 1).astype(bf16)

    sea_rows = []
    for read in (below, own, above):
        ind = read(slice(6 * CH, HALO))
        sea_rows += [ind[r : r + 1] for r in range(ROWS)]
    cell = lax.broadcasted_iota(jnp.int32, (CH, 2 * CH), 1)
    entry_at = lax.broadcasted_iota(jnp.int32, (CH, 2 * CH), 0)
    spread = (entry_at == (cell // CH) * 64 + (cell % CH) // 2).astype(f32)
    blocks = sum(warm_ref[(24 + i) * 8 : (25 + i) * 8, :] for i in range(8))
    on_cells = dot(blocks, spread, EXACT)
    warm = [[on_cells[i : i + 1, blk(r)] * ok[i] for r in range(2)] for i in range(3)]
    warm_adj = [[on_cells[3 + i : 4 + i, blk(r)] * ok[i] for r in range(2)] for i in range(3)]
    surface = [warm[r // 4][(r % 4) // 2] * sea_rows[r] for r in range(12)]

    for r in range(12):
        read = (below, own, above)[r // 4]
        value = read(blk(r % 4)) * ok[r // 4] + winj * surface[r]
        put_rolled(mixed_roll, r, value.astype(bf16).astype(f32))

    pre_first = dot(taps(k1_ref, 0), mixed_roll[:, blk(0, 10)])
    pre_first += dot(taps(k1_ref, 1), mixed_roll[:, blk(1, 10)])
    pre_first += dot(taps(k1_ref, 2), mixed_roll[:, blk(2, 10)])
    for i in range(10):
        act, slope = gelu_pair(pre_first[:, blk(i)])
        m = ok[(i + 1) // 4]
        put_rolled(act_roll, i, (act * m).astype(bf16).astype(f32))
        if 2 <= i < 8:
            slope_ref[:, blk(i - 2)] = slope * m

    state = dot(taps(k2_ref, 0), act_roll[:, blk(0, 8)])
    state += dot(taps(k2_ref, 1), act_roll[:, blk(1, 8)])
    state += dot(taps(k2_ref, 2), act_roll[:, blk(2, 8)])
    state_rows = []
    for i in range(8):
        row = (state[:, blk(i)] + mixed_roll[blk(1), blk(i + 2)].astype(f32)) * ok[(i + 2) // 4]
        state_rows.append(row.astype(bf16))
    state_b = jnp.concatenate(state_rows, axis=1)
    for r in range(ROWS):
        next_ref[blk(r), :] = state_rows[2 + r]

    flux = dot(proj_ref[...], state_b)
    even_lane = lax.broadcasted_iota(jnp.int32, (FX, CH), 1) % 2 == 0

    def pair_sum(v):
        return v + jnp.where(even_lane, pltpu.roll(v, CH - 1, 1), pltpu.roll(v, 1, 1))

    tile_flux, inv_count = [], []
    for q in range(4):
        sea_a, sea_b = sea_rows[2 + 2 * q], sea_rows[3 + 2 * q]
        count = pair_sum(jnp.broadcast_to(sea_a + sea_b, (FX, CH)))
        inv = 1.0 / jnp.maximum(count, 1.0)
        total = pair_sum(flux[:, blk(2 * q)] * sea_a + flux[:, blk(2 * q + 1)] * sea_b)
        tile_flux.append((total * inv).astype(bf16).astype(f32))
        inv_count.append(inv)
    block_flux = jnp.concatenate(tile_flux, axis=1)
    block_warm = jnp.concatenate([warm[0][1], warm[1][0], warm[1][1], warm[2][0]], axis=1)
    block_adj = jnp.concatenate(
        [warm_adj[0][1], warm_adj[1][0], warm_adj[1][1], warm_adj[2][0]], axis=1
    )

    ocean_in_ref[...] = jnp.zeros((24, 4 * CH), f32)
    ocean_in_ref[0:1, :] = block_warm
    ocean_in_ref[1:17, :] = block_flux
    entry_pad_ref[...] = jnp.zeros((24, CH), f32)
    entry_pad_ref[0:17, :] = entry_ref[...]
    pre_ocean = lax.dot_general(
        entry_pad_ref[...],
        ocean_in_ref[...],
        (((0,), (0,)), ((), ())),
        precision=EXACT,
        preferred_element_type=f32,
    )
    latent, ocean_slope = gelu_pair(pre_ocean)
    ocean_cot = exit_col * block_adj * ocean_slope
    flux_cot = dot(entry_ref[1:17, :], ocean_cot, EXACT)
    increment = jnp.sum(exit_col * latent[:, blk(1, 2)], axis=0, keepdims=True)
    increment = 0.5 * dot_nt(jnp.broadcast_to(increment, (16, 2 * CH)), spread, EXACT)
    small_ref[16:40, :] = 0.5 * dot_nt(ocean_in_ref[:, blk(1, 2)], ocean_cot[:, blk(1, 2)], EXACT)
    own_adj = jnp.broadcast_to(block_adj[:, blk(1, 2)], (8, 2 * CH))
    grad_out = 0.5 * dot_nt(own_adj, latent[:, blk(1, 2)], EXACT)

    fine_cot = jnp.concatenate(
        [flux_cot[:, blk(i // 2)] * inv_count[i // 2] * sea_rows[2 + i] for i in range(8)], axis=1
    )
    small_ref[0:16, :] = dot_nt(fine_cot[:, blk(2, 4)], state_b[:, blk(2, 4)].astype(f32), EXACT)
    back_flux = lax.dot_general(
        proj_ref[...].astype(f32),
        fine_cot,
        (((0,), (0,)), ((), ())),
        precision=EXACT,
        preferred_element_type=f32,
    )
    own_cot = []
    for i in range(8):
        at = blk(4 + i % 2)
        if i < 2:
            out_cot = below(at)
        elif i < 4:
            out_cot = jnp.where(even, far_ref[at, :].astype(f32), near_ref[at, :].astype(f32))
        elif i < 6:
            out_cot = jnp.where(even, near_ref[at, :].astype(f32), far_ref[at, :].astype(f32))
        else:
            out_cot = above(at)
        row = (out_cot + back_flux[:, blk(i)]) * ok[(i + 2) // 4]
        put_rolled(cot_roll, i, row.astype(bf16).astype(f32), True)
        if 2 <= i < 6:
            own_cot.append(row)

    def put_slab(s, value):
        if s < 15:
            pay_ref[blk(s), :] = value.astype(bf16)
        else:
            at = 24 * CHUNK + 2 * (s - 15) * CHUNK
            pay_ref[at : at + 64, :] = value[0:64].astype(bf16)
            pay_ref[at + CHUNK : at + CHUNK + 64, :] = value[64:128].astype(bf16)

    cot_own = cot_roll[blk(1), blk(2, 4)]
    for a in range(3):
        grad = dot_nt(cot_own, act_roll[:, blk(a + 2, 4)])
        for b in range(3):
            put_slab(9 + 3 * a + b, grad[:, blk(b)])

    act_cot = dot(k2b_ref[:, 0:384], cot_roll[:, blk(2, 6)])
    act_cot += dot(k2b_ref[:, 384:768], cot_roll[:, blk(1, 6)])
    act_cot += dot(k2b_ref[:, 768:1152], cot_roll[:, blk(0, 6)])
    for i in range(6):
        row = act_cot[:, blk(i)] * slope_ref[:, blk(i)]
        put_rolled(pre_roll, i, row.astype(bf16).astype(f32), True)

    pre_own = pre_roll[blk(1), blk(1, 4)]
    for a in range(3):
        grad = dot_nt(pre_own, mixed_roll[:, blk(a + 3, 4)])
        for b in range(3):
            put_slab(3 * a + b, grad[:, blk(b)])

    in_cot = jnp.concatenate(own_cot, axis=1)
    in_cot += dot(k1b_ref[:, 0:384], pre_roll[:, blk(2, 4)])
    in_cot += dot(k1b_ref[:, 384:768], pre_roll[:, blk(1, 4)])
    in_cot += dot(k1b_ref[:, 768:1152], pre_roll[:, blk(0, 4)])
    own_surface = jnp.broadcast_to(jnp.concatenate(surface[4:8], axis=1), (8, 4 * CH))
    grad_heat = dot_nt(own_surface, in_cot, EXACT)
    row_at = lax.broadcasted_iota(jnp.int32, (8, CH), 0)
    small_ref[40:48, :] = jnp.where(row_at == 0, grad_out[0:1], grad_heat[0:1])

    at = 30 * CHUNK
    pay_ref[at : at + 48, :] = small_ref[...].astype(bf16)
    pay_ref[at + 48 : at + 64, :] = jnp.zeros((16, CH), bf16)
    pay_ref[at + CHUNK : at + CHUNK + 64, :] = jnp.zeros((64, CH), bf16)
    for k in range(8):
        at = (24 + k) * CHUNK + 64
        pay_ref[at : at + 16, :] = increment.astype(bf16)


def run_step(*args):
    vmem = pl.BlockSpec(memory_space=pltpu.VMEM)
    return pl.pallas_call(
        step_kernel,
        out_shape=(
            jax.ShapeDtypeStruct((ROWS * CH, CH), bf16),
            jax.ShapeDtypeStruct((PAY, CH), bf16),
        ),
        in_specs=[vmem] * len(args),
        out_specs=(vmem, vmem),
        scratch_shapes=[
            pltpu.VMEM((3 * CH, 12 * CH), bf16),
            pltpu.VMEM((3 * CH, 10 * CH), bf16),
            pltpu.VMEM((3 * CH, 8 * CH), bf16),
            pltpu.VMEM((3 * CH, 6 * CH), bf16),
            pltpu.VMEM((CH, 6 * CH), f32),
            pltpu.VMEM((48, CH), f32),
            pltpu.VMEM((24, 4 * CH), f32),
            pltpu.VMEM((24, CH), f32),
        ],
        compiler_params=pltpu.CompilerParams(vmem_limit_bytes=32 * 1024 * 1024),
        cost_estimate=pl.CostEstimate(
            flops=1_500_000_000, bytes_accessed=4_000_000, transcendentals=300_000
        ),
    )(*args)


def prepare_kernel(
    flag_ref, air_ref, adj_ref, sea_ref, held_ref, near_ref, far_ref, rows
):
    turned = flag_ref[0] == 1
    even = lax.axis_index("core") == 0
    i = lax.broadcasted_iota(jnp.int32, (CH, CH), 0)
    j = lax.broadcasted_iota(jnp.int32, (CH, CH), 1)
    turn = jnp.where(i == jnp.where(turned, CH - 1 - j, j), 1.0, 0.0).astype(bf16)

    def canonical(ref):
        rows[...] = dot(ref[...], turn)
        stored = [rows[pl.ds(r, CH, stride=ROWS), :] for r in range(ROWS)]
        return [jnp.where(turned, stored[3 - r], stored[r]) for r in range(ROWS)]

    start = canonical(air_ref)
    for r in range(ROWS):
        near_ref[blk(r), :] = start[r].astype(bf16)
        far_ref[blk(r), :] = start[r].astype(bf16)
    cot = canonical(adj_ref)
    for r in range(2):
        near_ref[blk(4 + r), :] = jnp.where(even, cot[2 + r], cot[r]).astype(bf16)
        far_ref[blk(4 + r), :] = jnp.where(even, cot[r], cot[2 + r]).astype(bf16)
    sea = jnp.concatenate([sea_ref[0].astype(f32), jnp.zeros((12, CH), f32)], axis=0)
    near_ref[6 * CH : HALO, :] = sea.astype(bf16)
    far_ref[6 * CH : HALO, :] = sea.astype(bf16)


def hold_kernel(warm_ref, warm_adj_ref, held_ref):
    for r in range(LINES):
        held_ref[r : r + 1, :] = warm_ref[r]
        held_ref[16 + r : 17 + r, :] = warm_adj_ref[r]
    held_ref[15:16, :] = jnp.zeros((1, CH), f32)
    held_ref[31:32, :] = jnp.zeros((1, CH), f32)


def prepare(*args):
    vmem = pl.BlockSpec(memory_space=pltpu.VMEM)
    return pl.pallas_call(
        prepare_kernel,
        out_shape=(
            jax.ShapeDtypeStruct((HALO, CH), bf16),
            jax.ShapeDtypeStruct((HALO, CH), bf16),
        ),
        in_specs=[pl.BlockSpec(memory_space=pltpu.SMEM)] + [vmem] * (len(args) - 1),
        out_specs=(vmem, vmem),
        scratch_shapes=[pltpu.VMEM((ROWS * CH, CH), f32)],
        cost_estimate=pl.CostEstimate(
            flops=20_000_000_000, bytes_accessed=700_000, transcendentals=0
        ),
    )(*args)


def choose_kernel(parcel_ref, held_ref, far_ref, next_ref, last_ref, out_ref):
    zh, in_row = lax.axis_index("zh"), lax.axis_index("x") * 2 + lax.axis_index("core")
    here = jnp.where(zh == 3, 1.0, 0.0)
    table = held_ref[...] * here + far_ref[...] + next_ref[...] + last_ref[...]
    tile = lax.broadcasted_iota(jnp.int32, (TILES, 96), 0)
    lane = lax.broadcasted_iota(jnp.int32, (TILES, 96), 1)
    step, p = lane // 32, lane % 32
    wanted = (p // 8) * 32 + zh * 8 + p % 8 + step - 1
    pick = jnp.where(tile == wanted, 1.0, 0.0).astype(bf16)
    parcel = jnp.broadcast_to(parcel_ref[...], (16, TILES)).astype(f32).astype(bf16)
    line = dot(parcel, pick) - (in_row * LINES).astype(f32)
    at = lax.broadcasted_iota(jnp.int32, (16, 96), 0)
    chooser = jnp.where((at.astype(f32) == line) & (at < LINES), 1.0, 0.0)
    out_ref[...] = jnp.zeros((256, CH), f32)
    for field in range(2):
        rows = lax.dot_general(
            chooser,
            table[16 * field : 16 * field + 16],
            (((0,), (0,)), ((), ())),
            precision=EXACT,
            preferred_element_type=f32,
        )
        for step in range(3):
            out_ref[pl.ds(3 * field + step, 32, stride=8), :] = rows[step * 32 : step * 32 + 32]


def choose(*args):
    vmem = pl.BlockSpec(memory_space=pltpu.VMEM)
    return pl.pallas_call(
        choose_kernel,
        out_shape=jax.ShapeDtypeStruct((256, CH), f32),
        in_specs=[vmem] * len(args),
        out_specs=vmem,
        compiler_params=SMALL,
        cost_estimate=pl.CostEstimate(flops=20_000_000_000, bytes_accessed=200_000, transcendentals=0),
    )(*args)


def plane_sum_kernel(parcel_ref, parts_ref, out_ref):
    y, zh = lax.axis_index("y"), lax.axis_index("zh")
    first = (lax.axis_index("x") * 2 + lax.axis_index("core")) * LINES
    row = lax.broadcasted_iota(jnp.int32, (16, CH), 0)
    total = jnp.zeros((64, CH), f32)
    tail = jnp.zeros((16, CH), f32)
    lines = jnp.zeros((16, CH), f32)
    for p in range(32):
        total += parts_ref[p * CHUNK : p * CHUNK + 64, :].astype(f32)
        end = parts_ref[p * CHUNK + 64 : (p + 1) * CHUNK, :].astype(f32)
        tail += end
        tile = (p // 8) * 32 + zh * 8 + p % 8
        line = jnp.where(tile < AIR, parcel_ref[tile] - first, -1)
        lines += jnp.where((row == line) & (row < LINES), end, 0.0)
    tail = jnp.where(y == 3, lines, tail)
    for k in range(16):
        out_ref[k * CHUNK : k * CHUNK + 64, :] = total.astype(bf16)
        out_ref[k * CHUNK + 64 : (k + 1) * CHUNK, :] = tail.astype(bf16)


def column_sum_kernel(column_ref, sea_ref, out_ref, next_sea_ref):
    total = jnp.zeros((CHUNK, CH), f32)
    for k in range(16):
        total += column_ref[k * CHUNK : (k + 1) * CHUNK, :].astype(f32)
    total = (total * norm_scale).astype(bf16)
    for p in range(32):
        out_ref[p * CHUNK : (p + 1) * CHUNK, :] = total
    lines = jnp.zeros((16, CH), f32)
    for zh in range(4):
        at = pl.multiple_of((zh * 4 + lax.axis_index("mem")) * CHUNK + 64, 16)
        lines += column_ref[pl.ds(at, 16), :].astype(f32)
    ocean = jnp.where(tile_place() < AIR, 0.0, 1.0)
    for r in range(LINES):
        next_sea_ref[r] = (sea_ref[r] + lines[r : r + 1]) * ocean


def finish_kernel(whole_ref, lead_ref, close_ref, entry_ref, heat_ref, coupler_ref, exit_ref):
    def slab(s):
        if s < 15:
            return whole_ref[blk(s), :].astype(f32)
        at = 24 * CHUNK + 2 * (s - 15) * CHUNK
        halves = [whole_ref[at + k * CHUNK : at + k * CHUNK + 64, :] for k in range(2)]
        return jnp.concatenate(halves, axis=0).astype(f32)

    for s in range(9):
        lead_ref[blk(s), :] = slab(s)
        close_ref[blk(s), :] = slab(9 + s)
    small = whole_ref[30 * CHUNK : 30 * CHUNK + 48, :].astype(f32)
    coupler_ref[...] = small[0:16]
    entry_ref[...] = small[16:33]
    exit_ref[...] = small[40:41]
    heat_ref[...] = small[41:42]


def call(kernel, shapes, args, scalar=False, params=SMALL):
    vmem = pl.BlockSpec(memory_space=pltpu.VMEM)
    first = pl.BlockSpec(memory_space=pltpu.SMEM) if scalar else vmem
    return pl.pallas_call(
        kernel,
        out_shape=tuple(jax.ShapeDtypeStruct(*s) for s in shapes),
        in_specs=[first] + [vmem] * (len(args) - 1),
        out_specs=tuple(vmem for _ in shapes),
        compiler_params=params,
        cost_estimate=pl.CostEstimate(
            flops=2_000_000, bytes_accessed=1_000_000, transcendentals=0
        ),
    )(*args)


def exchange(value, axes):
    return lax.all_to_all(value, axes, 0, 0, tiled=True)


def local(
    air_fields,
    sea_warmth,
    rotation_flags,
    sea_pixel_indicator,
    panel_sea_parcel,
    opening_filter,
    closing_filter,
    warmth_injection,
    exchange_projection,
    sea_entry_matrix,
    sea_exit_matrix,
    air_adjoint_result,
    warmth_adjoint_result,
):
    sea_rows = sea_warmth.reshape(LINES, 1, CH)
    (held,) = call(
        hold_kernel,
        [((32, CH), f32)],
        (sea_rows, warmth_adjoint_result.reshape(LINES, 1, CH)),
        params=pltpu.CompilerParams(),
    )
    near_pay, far_pay = prepare(
        rotation_flags,
        air_fields.reshape(ROWS * CH, CH),
        air_adjoint_result.reshape(ROWS * CH, CH),
        sea_pixel_indicator,
        held,
    )

    reached = [lax.ppermute(held, ("y", "zh"), [(15, at)]) for at in (13, 12, 14)]
    swap = [(i, i ^ 1) for i in range(TILES)]
    from_near = lax.ppermute(near_pay, TILE_AXES, swap)
    swap = [(i, i + 1) for i in range(1, TILES - 1, 2)]
    from_far = lax.ppermute(far_pay, TILE_AXES, swap + [(j, i) for i, j in swap])
    leaving = choose(panel_sea_parcel.reshape(1, TILES), held, *reached)
    warm = exchange(leaving.reshape(32, 8, CH), PLANE).reshape(256, CH)

    def stacked(weights):
        return jnp.transpose(weights, (1, 2, 0, 3)).reshape(9 * CH, CH)

    flat = (CH, 9 * CH)
    next_rows, pay = run_step(
        warm,
        from_near,
        near_pay,
        far_pay,
        from_far,
        stacked(opening_filter),
        stacked(closing_filter),
        jnp.transpose(opening_filter, (3, 1, 2, 0)).reshape(flat),
        jnp.transpose(closing_filter, (3, 1, 2, 0)).reshape(flat),
        warmth_injection.reshape(1, CH),
        sea_exit_matrix.reshape(1, CH),
        exchange_projection,
        sea_entry_matrix.T,
    )

    parts = exchange(pay.reshape(32, CHUNK, CH), PLANE).reshape(PAY, CH)
    (column,) = call(
        plane_sum_kernel, [((16 * CHUNK, CH), bf16)], (panel_sea_parcel, parts), scalar=True
    )
    column = exchange(column.reshape(16, CHUNK, CH), ("zh", "mem")).reshape(16 * CHUNK, CH)
    total, next_sea = call(
        column_sum_kernel, [((PAY, CH), bf16), ((LINES, 1, CH), f32)], (column, sea_rows)
    )
    whole = exchange(total.reshape(32, CHUNK, CH), PLANE).reshape(PAY, CH)
    lead, close, entry, heat, coupler, exit_row = call(
        finish_kernel,
        [
            ((9 * CH, CH), f32),
            ((9 * CH, CH), f32),
            ((FX + 1, CH), f32),
            ((1, CH), f32),
            ((FX, CH), f32),
            ((1, CH), f32),
        ],
        (whole,),
    )

    def unstacked(rows):
        return jnp.transpose(rows.reshape(3, 3, CH, CH), (2, 0, 1, 3))

    flipped = rotation_flags[0] == 1
    next_air = jnp.transpose(next_rows.reshape(ROWS, CH, CH), (1, 0, 2))
    next_air = jnp.where(flipped, next_air[:, ::-1, ::-1], next_air)
    return (
        next_air[None, None],
        next_sea.reshape(1, 1, LINES, CH),
        unstacked(lead),
        unstacked(close),
        heat.reshape(CH),
        coupler,
        entry.T,
        exit_row.reshape(CH),
    )


def solution(mesh):
    fine = Mesh(mesh.devices.reshape(4, 4, 4, 4, 2), ("mem",) + TILE_AXES)
    tiles = P("mem", TILE_AXES)
    return jax.shard_map(
        local,
        mesh=fine,
        in_specs=(tiles, tiles, P(TILE_AXES), P(TILE_AXES))
        + (P(),) * 7
        + (tiles, tiles),
        out_specs=(tiles, tiles) + (P(),) * 6,
        check_vma=False,
    )
```

```python
import math

import jax
import jax.numpy as jnp
from jax import lax
from jax.experimental import pallas as pl
from jax.experimental.pallas import tpu as pltpu
from jax.sharding import Mesh, PartitionSpec as P

CH = 128
FX = 16
ROWS = 4
TILES = 128
AIR = 120
LINES = 15
CHUNK = 80
PAY = 32 * CHUNK
HALO = 6 * CH + 16
TILE_AXES = ("y", "zh", "x", "core")
PLANE = ("y", "x", "core")

gelu_scale = math.sqrt(2.0 / math.pi)
gelu_cubic = 0.044715
norm_scale = 1.0 / math.sqrt(4 * AIR * ROWS * CH)
EXACT = lax.Precision.HIGHEST
f32 = jnp.float32
SMALL = pltpu.CompilerParams(vmem_limit_bytes=12 * 1024 * 1024)
bf16 = jnp.bfloat16


def gelu_pair(value):
    square = value * value
    inner = gelu_scale * (value + gelu_cubic * square * value)
    tanh_val = jnp.tanh(inner)
    out = 0.5 * value * (1.0 + tanh_val)
    slope = 0.5 * (1.0 + tanh_val) + 0.5 * value * (1.0 - tanh_val * tanh_val) * gelu_scale * (
        1.0 + 3.0 * gelu_cubic * square
    )
    return (out, slope)


def dot(a, b, precision=None):
    return lax.dot_general(
        a, b, (((1,), (0,)), ((), ())), precision=precision, preferred_element_type=f32
    )


def dot_nt(a, b, precision=None):
    return lax.dot_general(
        a, b, (((1,), (1,)), ((), ())), precision=precision, preferred_element_type=f32
    )


def dot_tn(a, b):
    return lax.dot_general(a, b, (((0,), (0,)), ((), ())), preferred_element_type=f32)


def pieces(value, count=2):
    out = []
    for _ in range(count):
        out.append(value.astype(bf16))
        value = value - out[-1].astype(f32)
    return out


def stack(parts):
    return jnp.concatenate(parts, axis=0)


def folded(rows, n):
    return rows[0:n] + rows[n : 2 * n]


def blk(i, n=1):
    return slice(i * CH, (i + n) * CH)


def tile_place():
    y, zh, x, core = (lax.axis_index(a) for a in TILE_AXES)
    return ((y * 4 + zh) * 4 + x) * 2 + core


def two_parts(value):
    high = value.astype(bf16).astype(f32)
    return jnp.concatenate([high, value - high, jnp.zeros((16, CH), f32)], axis=0).astype(bf16)


def step_kernel(
    warm_ref,
    from_near_ref,
    near_ref,
    far_ref,
    from_far_ref,
    k1_ref,
    k2_ref,
    k1b_ref,
    k2b_ref,
    few_ref,
    next_ref,
    pay_ref,
    mixed_roll,
    act_roll,
    cot_roll,
    pre_roll,
    slope_ref,
    small_ref,
    ocean_in_ref,
):
    place = tile_place()
    mid = place < AIR
    ok = [jnp.where(t, 1.0, 0.0) for t in ((place > 0) & mid, mid, place < AIR - 1)]
    even = lax.axis_index("core") == 0
    cols = few_ref[0:8, :].T
    proj = few_ref[32:48, :].astype(bf16)
    winj, exit_col = cols[:, 0:1], cols[:, 1:2]

    def below(at):
        return jnp.where(even, from_far_ref[at, :].astype(f32), from_near_ref[at, :].astype(f32))

    def above(at):
        return jnp.where(even, from_near_ref[at, :].astype(f32), from_far_ref[at, :].astype(f32))

    def own(at):
        return near_ref[at, :].astype(f32)

    def taps(ref, a):
        return jnp.concatenate([ref[blk(3 * a + b), :] for b in range(3)], axis=1)

    def put_rolled(ref, i, value, back=False):
        ref[blk(0), blk(i)] = pltpu.roll(value, CH - 1 if back else 1, 1).astype(bf16)
        ref[blk(1), blk(i)] = value.astype(bf16)
        ref[blk(2), blk(i)] = pltpu.roll(value, 1 if back else CH - 1, 1).astype(bf16)

    sea_rows = []
    for read in (below, own, above):
        ind = read(slice(6 * CH, HALO))
        sea_rows += [ind[r : r + 1] for r in range(ROWS)]
    cell = lax.broadcasted_iota(jnp.int32, (CH, 2 * CH), 1)
    entry_at = lax.broadcasted_iota(jnp.int32, (CH, 2 * CH), 0)
    spread = (entry_at == (cell // CH) * 64 + (cell % CH) // 2).astype(bf16)
    blocks = sum(warm_ref[(24 + i) * 8 : (25 + i) * 8, :] for i in range(8))
    on_cells = dot(blocks, spread.astype(f32), EXACT)
    warm = [[on_cells[i : i + 1, blk(r)] * ok[i] for r in range(2)] for i in range(3)]
    warm_adj = [[on_cells[3 + i : 4 + i, blk(r)] * ok[i] for r in range(2)] for i in range(3)]
    surface = [warm[r // 4][(r % 4) // 2] * sea_rows[r] for r in range(12)]

    for r in range(12):
        read = (below, own, above)[r // 4]
        value = read(blk(r % 4)) * ok[r // 4] + winj * surface[r]
        put_rolled(mixed_roll, r, value.astype(bf16).astype(f32))

    pre_first = dot(taps(k1_ref, 0), mixed_roll[:, blk(0, 10)])
    pre_first += dot(taps(k1_ref, 1), mixed_roll[:, blk(1, 10)])
    pre_first += dot(taps(k1_ref, 2), mixed_roll[:, blk(2, 10)])
    for i in range(10):
        act, slope = gelu_pair(pre_first[:, blk(i)])
        m = ok[(i + 1) // 4]
        put_rolled(act_roll, i, (act * m).astype(bf16).astype(f32))
        if 2 <= i < 8:
            slope_ref[:, blk(i - 2)] = slope * m

    state = dot(taps(k2_ref, 0), act_roll[:, blk(0, 8)])
    state += dot(taps(k2_ref, 1), act_roll[:, blk(1, 8)])
    state += dot(taps(k2_ref, 2), act_roll[:, blk(2, 8)])
    state_rows = []
    for i in range(8):
        row = (state[:, blk(i)] + mixed_roll[blk(1), blk(i + 2)].astype(f32)) * ok[(i + 2) // 4]
        state_rows.append(row.astype(bf16))
    state_b = jnp.concatenate(state_rows, axis=1)
    for r in range(ROWS):
        next_ref[blk(r), :] = state_rows[2 + r]

    flux = dot(proj, state_b)
    even_lane = lax.broadcasted_iota(jnp.int32, (FX, CH), 1) % 2 == 0

    def pair_sum(v):
        return v + jnp.where(even_lane, pltpu.roll(v, CH - 1, 1), pltpu.roll(v, 1, 1))

    tile_flux, inv_count = [], []
    for q in range(4):
        sea_a, sea_b = sea_rows[2 + 2 * q], sea_rows[3 + 2 * q]
        count = pair_sum(jnp.broadcast_to(sea_a + sea_b, (FX, CH)))
        inv = 1.0 / jnp.maximum(count, 1.0)
        total = pair_sum(flux[:, blk(2 * q)] * sea_a + flux[:, blk(2 * q + 1)] * sea_b)
        tile_flux.append((total * inv).astype(bf16).astype(f32))
        inv_count.append(inv)
    block_flux = jnp.concatenate(tile_flux, axis=1)
    block_warm = jnp.concatenate([warm[0][1], warm[1][0], warm[1][1], warm[2][0]], axis=1)
    block_adj = jnp.concatenate(
        [warm_adj[0][1], warm_adj[1][0], warm_adj[1][1], warm_adj[2][0]], axis=1
    )

    ocean_in_ref[...] = jnp.zeros((24, 4 * CH), f32)
    ocean_in_ref[0:1, :] = block_warm
    ocean_in_ref[1:17, :] = block_flux
    entry_hi, entry_lo = pieces(few_ref[8:32, :])
    in_hi, in_lo = pieces(ocean_in_ref[...])
    zero = jnp.zeros((8, CH), bf16)
    pre_ocean = dot_tn(
        stack([entry_hi, entry_lo, entry_hi, zero]),
        stack([in_hi, in_hi, in_lo, jnp.zeros((8, 4 * CH), bf16)]),
    )
    latent, ocean_slope = gelu_pair(pre_ocean)
    ocean_cot = exit_col * block_adj * ocean_slope
    cot_hi, cot_lo = pieces(ocean_cot)
    entry_hi, entry_lo = pieces(few_ref[9:25, :])
    flux_cot = folded(dot(stack([entry_hi, entry_lo]), cot_hi), 16) + dot(entry_hi, cot_lo)
    increment = jnp.sum(exit_col * latent[:, blk(1, 2)], axis=0, keepdims=True)
    increment = stack(pieces(jnp.broadcast_to(increment, (16, 2 * CH))))
    increment = 0.5 * folded(dot_nt(increment, spread), 16)
    own_in = stack([in_hi, in_lo])[:, blk(1, 2)]
    grad_in = folded(dot_nt(own_in, cot_hi[:, blk(1, 2)]), 24)
    grad_in += dot_nt(in_hi[:, blk(1, 2)], cot_lo[:, blk(1, 2)])
    small_ref[16:40, :] = 0.5 * grad_in
    own_adj = jnp.broadcast_to(block_adj[:, blk(1, 2)], (8, 2 * CH))
    own_adj = stack(pieces(own_adj))
    lat_hi, lat_lo = pieces(latent[:, blk(1, 2)])
    grad_out = 0.5 * (folded(dot_nt(own_adj, lat_hi), 8) + dot_nt(own_adj, lat_lo)[0:8])

    fine_cot = jnp.concatenate(
        [flux_cot[:, blk(i // 2)] * inv_count[i // 2] * sea_rows[2 + i] for i in range(8)], axis=1
    )
    fine_parts = stack(pieces(fine_cot))
    small_ref[0:16, :] = folded(dot_nt(fine_parts[:, blk(2, 4)], state_b[:, blk(2, 4)]), 16)
    back_flux = dot_tn(stack([proj, proj]), fine_parts)
    own_cot = []
    for i in range(8):
        at = blk(4 + i % 2)
        if i < 2:
            out_cot = below(at)
        elif i < 4:
            out_cot = jnp.where(even, far_ref[at, :].astype(f32), near_ref[at, :].astype(f32))
        elif i < 6:
            out_cot = jnp.where(even, near_ref[at, :].astype(f32), far_ref[at, :].astype(f32))
        else:
            out_cot = above(at)
        row = (out_cot + back_flux[:, blk(i)]) * ok[(i + 2) // 4]
        put_rolled(cot_roll, i, row.astype(bf16).astype(f32), True)
        if 2 <= i < 6:
            own_cot.append(row)

    def put_slab(s, value):
        if s < 15:
            pay_ref[blk(s), :] = value.astype(bf16)
        else:
            at = 24 * CHUNK + 2 * (s - 15) * CHUNK
            pay_ref[at : at + 64, :] = value[0:64].astype(bf16)
            pay_ref[at + CHUNK : at + CHUNK + 64, :] = value[64:128].astype(bf16)

    cot_own = cot_roll[blk(1), blk(2, 4)]
    for a in range(3):
        grad = dot_nt(cot_own, act_roll[:, blk(a + 2, 4)])
        for b in range(3):
            put_slab(9 + 3 * a + b, grad[:, blk(b)])

    act_cot = dot(k2b_ref[:, 0:384], cot_roll[:, blk(2, 6)])
    act_cot += dot(k2b_ref[:, 384:768], cot_roll[:, blk(1, 6)])
    act_cot += dot(k2b_ref[:, 768:1152], cot_roll[:, blk(0, 6)])
    for i in range(6):
        row = act_cot[:, blk(i)] * slope_ref[:, blk(i)]
        put_rolled(pre_roll, i, row.astype(bf16).astype(f32), True)

    pre_own = pre_roll[blk(1), blk(1, 4)]
    for a in range(3):
        grad = dot_nt(pre_own, mixed_roll[:, blk(a + 3, 4)])
        for b in range(3):
            put_slab(3 * a + b, grad[:, blk(b)])

    in_cot = jnp.concatenate(own_cot, axis=1)
    in_cot += dot(k1b_ref[:, 0:384], pre_roll[:, blk(2, 4)])
    in_cot += dot(k1b_ref[:, 384:768], pre_roll[:, blk(1, 4)])
    in_cot += dot(k1b_ref[:, 768:1152], pre_roll[:, blk(0, 4)])
    own_surface = jnp.broadcast_to(jnp.concatenate(surface[4:8], axis=1), (8, 4 * CH))
    own_surface = stack(pieces(own_surface))
    in_hi, in_lo = pieces(in_cot)
    grad_heat = folded(dot_nt(own_surface, in_hi), 8) + dot_nt(own_surface, in_lo)[0:8]
    row_at = lax.broadcasted_iota(jnp.int32, (8, CH), 0)
    small_ref[40:48, :] = jnp.where(row_at == 0, grad_out[0:1], grad_heat[0:1])

    for k in range(2):
        at = (30 + k) * CHUNK
        pay_ref[at : at + 64, :] = two_parts(small_ref[24 * k : 24 * k + 24, :])
    for k in range(8):
        at = (24 + k) * CHUNK + 64
        pay_ref[at : at + 16, :] = increment.astype(bf16)


def run_step(*args):
    vmem = pl.BlockSpec(memory_space=pltpu.VMEM)
    return pl.pallas_call(
        step_kernel,
        out_shape=(
            jax.ShapeDtypeStruct((ROWS * CH, CH), bf16),
            jax.ShapeDtypeStruct((PAY, CH), bf16),
        ),
        in_specs=[vmem] * len(args),
        out_specs=(vmem, vmem),
        scratch_shapes=[
            pltpu.VMEM((3 * CH, 12 * CH), bf16),
            pltpu.VMEM((3 * CH, 10 * CH), bf16),
            pltpu.VMEM((3 * CH, 8 * CH), bf16),
            pltpu.VMEM((3 * CH, 6 * CH), bf16),
            pltpu.VMEM((CH, 6 * CH), f32),
            pltpu.VMEM((48, CH), f32),
            pltpu.VMEM((24, 4 * CH), f32),
        ],
        compiler_params=pltpu.CompilerParams(vmem_limit_bytes=32 * 1024 * 1024),
        cost_estimate=pl.CostEstimate(
            flops=1_500_000_000, bytes_accessed=4_000_000, transcendentals=300_000
        ),
    )(*args)


def hold(warm_ref, warm_adj_ref, held_ref):
    for r in range(LINES):
        held_ref[r : r + 1, :] = warm_ref[r]
        held_ref[16 + r : 17 + r, :] = warm_adj_ref[r]
    held_ref[15:16, :] = jnp.zeros((1, CH), f32)
    held_ref[31:32, :] = jnp.zeros((1, CH), f32)


def prepare_kernel(
    flag_ref, air_ref, adj_ref, sea_ref, warm_ref, warm_adj_ref, near_ref, far_ref, held_ref, rows
):
    turned = flag_ref[0] == 1
    even = lax.axis_index("core") == 0
    i = lax.broadcasted_iota(jnp.int32, (CH, CH), 0)
    j = lax.broadcasted_iota(jnp.int32, (CH, CH), 1)
    turn = jnp.where(i == jnp.where(turned, CH - 1 - j, j), 1.0, 0.0).astype(bf16)

    def canonical(ref):
        rows[...] = dot(ref[...], turn)
        stored = [rows[pl.ds(r, CH, stride=ROWS), :] for r in range(ROWS)]
        return [jnp.where(turned, stored[3 - r], stored[r]) for r in range(ROWS)]

    hold(warm_ref, warm_adj_ref, held_ref)
    start = canonical(air_ref)
    for r in range(ROWS):
        near_ref[blk(r), :] = start[r].astype(bf16)
        far_ref[blk(r), :] = start[r].astype(bf16)
    cot = canonical(adj_ref)
    for r in range(2):
        near_ref[blk(4 + r), :] = jnp.where(even, cot[2 + r], cot[r]).astype(bf16)
        far_ref[blk(4 + r), :] = jnp.where(even, cot[r], cot[2 + r]).astype(bf16)
    sea = jnp.concatenate([sea_ref[0].astype(f32), jnp.zeros((12, CH), f32)], axis=0)
    near_ref[6 * CH : HALO, :] = sea.astype(bf16)
    far_ref[6 * CH : HALO, :] = sea.astype(bf16)


def prepare(*args):
    vmem = pl.BlockSpec(memory_space=pltpu.VMEM)
    return pl.pallas_call(
        prepare_kernel,
        out_shape=(
            jax.ShapeDtypeStruct((HALO, CH), bf16),
            jax.ShapeDtypeStruct((HALO, CH), bf16),
            jax.ShapeDtypeStruct((32, CH), f32),
        ),
        in_specs=[pl.BlockSpec(memory_space=pltpu.SMEM)] + [vmem] * (len(args) - 1),
        out_specs=(vmem, vmem, vmem),
        scratch_shapes=[pltpu.VMEM((ROWS * CH, CH), f32)],
        cost_estimate=pl.CostEstimate(
            flops=20_000_000_000, bytes_accessed=700_000, transcendentals=0
        ),
    )(*args)


def choose_kernel(parcel_ref, warm_ref, warm_adj_ref, far_ref, next_ref, last_ref, out_ref, held_ref):
    zh, in_row = lax.axis_index("zh"), lax.axis_index("x") * 2 + lax.axis_index("core")
    here = jnp.where(zh == 3, 1.0, 0.0)
    hold(warm_ref, warm_adj_ref, held_ref)
    tile = lax.broadcasted_iota(jnp.int32, (TILES, 96), 0)
    lane = lax.broadcasted_iota(jnp.int32, (TILES, 96), 1)
    step, p = lane // 32, lane % 32
    wanted = (p // 8) * 32 + zh * 8 + p % 8 + step - 1
    pick = jnp.where(tile == wanted, 1.0, 0.0).astype(bf16)
    parcel = jnp.broadcast_to(parcel_ref[...], (16, TILES)).astype(f32).astype(bf16)
    line = dot(parcel, pick) - (in_row * LINES).astype(f32)
    at = lax.broadcasted_iota(jnp.int32, (16, 96), 0)
    chooser = jnp.where((at.astype(f32) == line) & (at < LINES), 1.0, 0.0).astype(bf16)
    chooser = stack([chooser] * 3)
    out_ref[...] = jnp.zeros((256, CH), f32)
    table = held_ref[...] * here + far_ref[...] + next_ref[...] + last_ref[...]
    for field in range(2):
        rows = dot_tn(chooser, stack(pieces(table[16 * field : 16 * field + 16], 3)))
        for step in range(3):
            out_ref[pl.ds(3 * field + step, 32, stride=8), :] = rows[step * 32 : step * 32 + 32]


def choose(*args):
    vmem = pl.BlockSpec(memory_space=pltpu.VMEM)
    return pl.pallas_call(
        choose_kernel,
        out_shape=jax.ShapeDtypeStruct((256, CH), f32),
        in_specs=[vmem] * len(args),
        out_specs=vmem,
        scratch_shapes=[pltpu.VMEM((32, CH), f32)],
        compiler_params=SMALL,
        cost_estimate=pl.CostEstimate(flops=20_000_000_000, bytes_accessed=200_000, transcendentals=0),
    )(*args)


def plane_sum_kernel(parcel_ref, parts_ref, out_ref):
    y, zh = lax.axis_index("y"), lax.axis_index("zh")
    first = (lax.axis_index("x") * 2 + lax.axis_index("core")) * LINES
    row = lax.broadcasted_iota(jnp.int32, (16, CH), 0)
    total = jnp.zeros((64, CH), f32)
    tail = jnp.zeros((16, CH), f32)
    lines = jnp.zeros((16, CH), f32)
    for p in range(32):
        total += parts_ref[p * CHUNK : p * CHUNK + 64, :].astype(f32)
        end = parts_ref[p * CHUNK + 64 : (p + 1) * CHUNK, :].astype(f32)
        tail += end
        tile = (p // 8) * 32 + zh * 8 + p % 8
        line = jnp.where(tile < AIR, parcel_ref[tile] - first, -1)
        lines += jnp.where((row == line) & (row < LINES), end, 0.0)
    tail = jnp.where(y == 3, lines, tail)
    split = two_parts(total[0:24] + total[24:48]).astype(f32)
    total = jnp.where((y == 3) & (lax.axis_index("x") == 3), split, total)
    for k in range(16):
        out_ref[k * CHUNK : k * CHUNK + 64, :] = total.astype(bf16)
        out_ref[k * CHUNK + 64 : (k + 1) * CHUNK, :] = tail.astype(bf16)


def column_sum_kernel(column_ref, sea_ref, out_ref, next_sea_ref):
    total = jnp.zeros((CHUNK, CH), f32)
    for k in range(16):
        total += column_ref[k * CHUNK : (k + 1) * CHUNK, :].astype(f32)
    total = total * norm_scale
    split = two_parts(total[0:24] + total[24:48]).astype(f32)
    is_small = (lax.axis_index("y") == 3) & (lax.axis_index("x") == 3)
    head = jnp.where(is_small, split, total[0:64]).astype(bf16)
    tail = total[64:CHUNK].astype(bf16)
    for p in range(32):
        out_ref[p * CHUNK : p * CHUNK + 64, :] = head
        out_ref[p * CHUNK + 64 : (p + 1) * CHUNK, :] = tail
    lines = jnp.zeros((16, CH), f32)
    for zh in range(4):
        at = pl.multiple_of((zh * 4 + lax.axis_index("mem")) * CHUNK + 64, 16)
        lines += column_ref[pl.ds(at, 16), :].astype(f32)
    ocean = jnp.where(tile_place() < AIR, 0.0, 1.0)
    for r in range(LINES):
        next_sea_ref[r] = (sea_ref[r] + lines[r : r + 1]) * ocean


def finish_kernel(whole_ref, lead_ref, close_ref, entry_ref, heat_ref, coupler_ref, exit_ref):
    def slab(s):
        if s < 15:
            return whole_ref[blk(s), :].astype(f32)
        at = 24 * CHUNK + 2 * (s - 15) * CHUNK
        halves = [whole_ref[at + k * CHUNK : at + k * CHUNK + 64, :] for k in range(2)]
        return jnp.concatenate(halves, axis=0).astype(f32)

    for s in range(9):
        lead_ref[blk(s), :] = slab(s)
        close_ref[blk(s), :] = slab(9 + s)
    small = []
    for k in range(2):
        parts = whole_ref[(30 + k) * CHUNK : (30 + k) * CHUNK + 48, :].astype(f32)
        small.append(parts[0:24] + parts[24:48])
    small = jnp.concatenate(small, axis=0)
    coupler_ref[...] = small[0:16]
    entry_ref[...] = small[16:33]
    exit_ref[...] = small[40:41]
    heat_ref[...] = small[41:42]


def call(kernel, shapes, args, scalar=False, params=SMALL):
    vmem = pl.BlockSpec(memory_space=pltpu.VMEM)
    first = pl.BlockSpec(memory_space=pltpu.SMEM) if scalar else vmem
    return pl.pallas_call(
        kernel,
        out_shape=tuple(jax.ShapeDtypeStruct(*s) for s in shapes),
        in_specs=[first] + [vmem] * (len(args) - 1),
        out_specs=tuple(vmem for _ in shapes),
        compiler_params=params,
        cost_estimate=pl.CostEstimate(
            flops=2_000_000, bytes_accessed=1_000_000, transcendentals=0
        ),
    )(*args)


def exchange(value, axes):
    return lax.all_to_all(value, axes, 0, 0, tiled=True)


def local(
    air_fields,
    sea_warmth,
    rotation_flags,
    sea_pixel_indicator,
    panel_sea_parcel,
    opening_filter,
    closing_filter,
    warmth_injection,
    exchange_projection,
    sea_entry_matrix,
    sea_exit_matrix,
    air_adjoint_result,
    warmth_adjoint_result,
):
    sea_rows = sea_warmth.reshape(LINES, 1, CH)
    adj_rows = warmth_adjoint_result.reshape(LINES, 1, CH)
    near_pay, far_pay, held = prepare(
        rotation_flags,
        air_fields.reshape(ROWS * CH, CH),
        air_adjoint_result.reshape(ROWS * CH, CH),
        sea_pixel_indicator,
        sea_rows,
        adj_rows,
    )

    reached = [lax.ppermute(held, ("y", "zh"), [(15, at)]) for at in (14, 13, 12)]
    swap = [(i, i ^ 1) for i in range(TILES)]
    from_near = lax.ppermute(near_pay, TILE_AXES, swap)
    swap = [(i, i + 1) for i in range(1, TILES - 1, 2)]
    from_far = lax.ppermute(far_pay, TILE_AXES, swap + [(j, i) for i, j in swap])
    leaving = choose(panel_sea_parcel.reshape(1, TILES), sea_rows, adj_rows, *reached)
    warm = exchange(leaving.reshape(32, 8, CH), PLANE).reshape(256, CH)

    def stacked(weights):
        return jnp.transpose(weights, (1, 2, 0, 3)).reshape(9 * CH, CH)

    few = jnp.concatenate(
        [
            warmth_injection[None],
            sea_exit_matrix[None],
            jnp.zeros((6, CH), f32),
            sea_entry_matrix.T,
            jnp.zeros((7, CH), f32),
            exchange_projection.astype(f32),
        ]
    )
    flat = (CH, 9 * CH)
    next_rows, pay = run_step(
        warm,
        from_near,
        near_pay,
        far_pay,
        from_far,
        stacked(opening_filter),
        stacked(closing_filter),
        jnp.transpose(opening_filter, (3, 1, 2, 0)).reshape(flat),
        jnp.transpose(closing_filter, (3, 1, 2, 0)).reshape(flat),
        few,
    )

    parts = exchange(pay.reshape(32, CHUNK, CH), PLANE).reshape(PAY, CH)
    (column,) = call(
        plane_sum_kernel, [((16 * CHUNK, CH), bf16)], (panel_sea_parcel, parts), scalar=True
    )
    column = exchange(column.reshape(16, CHUNK, CH), ("zh", "mem")).reshape(16 * CHUNK, CH)
    total, next_sea = call(
        column_sum_kernel, [((PAY, CH), bf16), ((LINES, 1, CH), f32)], (column, sea_rows)
    )
    whole = exchange(total.reshape(32, CHUNK, CH), PLANE).reshape(PAY, CH)
    lead, close, entry, heat, coupler, exit_row = call(
        finish_kernel,
        [
            ((9 * CH, CH), f32),
            ((9 * CH, CH), f32),
            ((FX + 1, CH), f32),
            ((1, CH), f32),
            ((FX, CH), f32),
            ((1, CH), f32),
        ],
        (whole,),
    )

    def unstacked(rows):
        return jnp.transpose(rows.reshape(3, 3, CH, CH), (2, 0, 1, 3))

    flipped = rotation_flags[0] == 1
    next_air = jnp.transpose(next_rows.reshape(ROWS, CH, CH), (1, 0, 2))
    next_air = jnp.where(flipped, next_air[:, ::-1, ::-1], next_air)
    return (
        next_air[None, None],
        next_sea.reshape(1, 1, LINES, CH),
        unstacked(lead),
        unstacked(close),
        heat.reshape(CH),
        coupler,
        entry.T,
        exit_row.reshape(CH),
    )


def solution(mesh):
    fine = Mesh(mesh.devices.reshape(4, 4, 4, 4, 2), ("mem",) + TILE_AXES)
    tiles = P("mem", TILE_AXES)
    return jax.shard_map(
        local,
        mesh=fine,
        in_specs=(tiles, tiles, P(TILE_AXES), P(TILE_AXES))
        + (P(),) * 7
        + (tiles, tiles),
        out_specs=(tiles, tiles) + (P(),) * 6,
        check_vma=False,
    )
```

```python
import math

import jax
import jax.numpy as jnp
from jax import lax
from jax.experimental import pallas as pl
from jax.experimental.pallas import tpu as pltpu
from jax.sharding import Mesh, PartitionSpec as P

CH = 128
FX = 16
ROWS = 4
TILES = 128
AIR = 120
LINES = 15
CHUNK = 48
PAY = 64 * CHUNK
HALO = 6 * CH + 16
TILE_AXES = ("y", "zh", "x", "core")
PLANE = ("y", "x", "core")
PAIR = ("m0",) + PLANE

gelu_scale = math.sqrt(2.0 / math.pi)
gelu_cubic = 0.044715
norm_scale = 1.0 / math.sqrt(4 * AIR * ROWS * CH)
EXACT = lax.Precision.HIGHEST
f32 = jnp.float32
SMALL = pltpu.CompilerParams(vmem_limit_bytes=12 * 1024 * 1024)
bf16 = jnp.bfloat16


def gelu_pair(value):
    square = value * value
    inner = gelu_scale * (value + gelu_cubic * square * value)
    tanh_val = jnp.tanh(inner)
    out = 0.5 * value * (1.0 + tanh_val)
    slope = 0.5 * (1.0 + tanh_val) + 0.5 * value * (1.0 - tanh_val * tanh_val) * gelu_scale * (
        1.0 + 3.0 * gelu_cubic * square
    )
    return (out, slope)


def dot(a, b, precision=None):
    return lax.dot_general(
        a, b, (((1,), (0,)), ((), ())), precision=precision, preferred_element_type=f32
    )


def dot_nt(a, b, precision=None):
    return lax.dot_general(
        a, b, (((1,), (1,)), ((), ())), precision=precision, preferred_element_type=f32
    )


def dot_tn(a, b):
    return lax.dot_general(a, b, (((0,), (0,)), ((), ())), preferred_element_type=f32)


def pieces(value, count=2):
    out = []
    for _ in range(count):
        out.append(value.astype(bf16))
        value = value - out[-1].astype(f32)
    return out


def stack(parts):
    return jnp.concatenate(parts, axis=0)


def folded(rows, n):
    return rows[0:n] + rows[n : 2 * n]


def blk(i, n=1):
    return slice(i * CH, (i + n) * CH)


def tile_place():
    y, zh, x, core = (lax.axis_index(a) for a in TILE_AXES)
    return ((y * 4 + zh) * 4 + x) * 2 + core


def two_parts(value):
    high = value.astype(bf16).astype(f32)
    return jnp.concatenate([high, value - high], axis=0)


def parts_again(total, is_small):
    split = two_parts(total[0:16] + total[16:32])
    return jnp.where(is_small, split, total[0:32]).astype(bf16)


def step_kernel(
    warm_ref,
    from_near_ref,
    near_ref,
    far_ref,
    from_far_ref,
    k1_ref,
    k2_ref,
    k1b_ref,
    k2b_ref,
    few_ref,
    next_ref,
    pay_ref,
    mixed_roll,
    act_roll,
    cot_roll,
    pre_roll,
    slope_ref,
    small_ref,
    ocean_in_ref,
):
    place = tile_place()
    mid = place < AIR
    ok = [jnp.where(t, 1.0, 0.0) for t in ((place > 0) & mid, mid, place < AIR - 1)]
    even = lax.axis_index("core") == 0
    cols = few_ref[0:8, :].T
    proj = few_ref[32:48, :].astype(bf16)
    winj, exit_col = cols[:, 0:1], cols[:, 1:2]

    def below(at):
        return jnp.where(even, from_far_ref[at, :].astype(f32), from_near_ref[at, :].astype(f32))

    def above(at):
        return jnp.where(even, from_near_ref[at, :].astype(f32), from_far_ref[at, :].astype(f32))

    def own(at):
        return near_ref[at, :].astype(f32)

    def taps(ref, a):
        return jnp.concatenate([ref[blk(3 * a + b), :] for b in range(3)], axis=1)

    def put_rolled(ref, i, value, back=False):
        ref[blk(0), blk(i)] = pltpu.roll(value, CH - 1 if back else 1, 1).astype(bf16)
        ref[blk(1), blk(i)] = value.astype(bf16)
        ref[blk(2), blk(i)] = pltpu.roll(value, 1 if back else CH - 1, 1).astype(bf16)

    sea_rows = []
    for read in (below, own, above):
        ind = read(slice(6 * CH, HALO))
        sea_rows += [ind[r : r + 1] for r in range(ROWS)]
    cell = lax.broadcasted_iota(jnp.int32, (CH, 2 * CH), 1)
    entry_at = lax.broadcasted_iota(jnp.int32, (CH, 2 * CH), 0)
    spread = (entry_at == (cell // CH) * 64 + (cell % CH) // 2).astype(bf16)
    blocks = sum(warm_ref[(24 + i) * 8 : (25 + i) * 8, :] for i in range(8))
    on_cells = dot(blocks, spread.astype(f32), EXACT)
    warm = [[on_cells[i : i + 1, blk(r)] * ok[i] for r in range(2)] for i in range(3)]
    warm_adj = [[on_cells[3 + i : 4 + i, blk(r)] * ok[i] for r in range(2)] for i in range(3)]
    surface = [warm[r // 4][(r % 4) // 2] * sea_rows[r] for r in range(12)]

    for r in range(12):
        read = (below, own, above)[r // 4]
        value = read(blk(r % 4)) * ok[r // 4] + winj * surface[r]
        put_rolled(mixed_roll, r, value.astype(bf16).astype(f32))

    pre_first = dot(taps(k1_ref, 0), mixed_roll[:, blk(0, 10)])
    pre_first += dot(taps(k1_ref, 1), mixed_roll[:, blk(1, 10)])
    pre_first += dot(taps(k1_ref, 2), mixed_roll[:, blk(2, 10)])
    for i in range(10):
        act, slope = gelu_pair(pre_first[:, blk(i)])
        m = ok[(i + 1) // 4]
        put_rolled(act_roll, i, (act * m).astype(bf16).astype(f32))
        if 2 <= i < 8:
            slope_ref[:, blk(i - 2)] = slope * m

    state = dot(taps(k2_ref, 0), act_roll[:, blk(0, 8)])
    state += dot(taps(k2_ref, 1), act_roll[:, blk(1, 8)])
    state += dot(taps(k2_ref, 2), act_roll[:, blk(2, 8)])
    state_rows = []
    for i in range(8):
        row = (state[:, blk(i)] + mixed_roll[blk(1), blk(i + 2)].astype(f32)) * ok[(i + 2) // 4]
        state_rows.append(row.astype(bf16))
    state_b = jnp.concatenate(state_rows, axis=1)
    for r in range(ROWS):
        next_ref[blk(r), :] = state_rows[2 + r]

    flux = dot(proj, state_b)
    even_lane = lax.broadcasted_iota(jnp.int32, (FX, CH), 1) % 2 == 0

    def pair_sum(v):
        return v + jnp.where(even_lane, pltpu.roll(v, CH - 1, 1), pltpu.roll(v, 1, 1))

    tile_flux, inv_count = [], []
    for q in range(4):
        sea_a, sea_b = sea_rows[2 + 2 * q], sea_rows[3 + 2 * q]
        count = pair_sum(jnp.broadcast_to(sea_a + sea_b, (FX, CH)))
        inv = 1.0 / jnp.maximum(count, 1.0)
        total = pair_sum(flux[:, blk(2 * q)] * sea_a + flux[:, blk(2 * q + 1)] * sea_b)
        tile_flux.append((total * inv).astype(bf16).astype(f32))
        inv_count.append(inv)
    block_flux = jnp.concatenate(tile_flux, axis=1)
    block_warm = jnp.concatenate([warm[0][1], warm[1][0], warm[1][1], warm[2][0]], axis=1)
    block_adj = jnp.concatenate(
        [warm_adj[0][1], warm_adj[1][0], warm_adj[1][1], warm_adj[2][0]], axis=1
    )

    ocean_in_ref[...] = jnp.zeros((24, 4 * CH), f32)
    ocean_in_ref[0:1, :] = block_warm
    ocean_in_ref[1:17, :] = block_flux
    entry_hi, entry_lo = pieces(few_ref[8:32, :])
    in_hi, in_lo = pieces(ocean_in_ref[...])
    zero = jnp.zeros((8, CH), bf16)
    pre_ocean = dot_tn(
        stack([entry_hi, entry_lo, entry_hi, zero]),
        stack([in_hi, in_hi, in_lo, jnp.zeros((8, 4 * CH), bf16)]),
    )
    latent, ocean_slope = gelu_pair(pre_ocean)
    ocean_cot = exit_col * block_adj * ocean_slope
    cot_hi, cot_lo = pieces(ocean_cot)
    entry_hi, entry_lo = pieces(few_ref[9:25, :])
    flux_cot = folded(dot(stack([entry_hi, entry_lo]), cot_hi), 16) + dot(entry_hi, cot_lo)
    increment = jnp.sum(exit_col * latent[:, blk(1, 2)], axis=0, keepdims=True)
    increment = stack(pieces(jnp.broadcast_to(increment, (16, 2 * CH))))
    increment = 0.5 * folded(dot_nt(increment, spread), 16)
    own_in = stack([in_hi, in_lo])[:, blk(1, 2)]
    grad_in = folded(dot_nt(own_in, cot_hi[:, blk(1, 2)]), 24)
    grad_in += dot_nt(in_hi[:, blk(1, 2)], cot_lo[:, blk(1, 2)])
    small_ref[16:40, :] = 0.5 * grad_in
    own_adj = jnp.broadcast_to(block_adj[:, blk(1, 2)], (8, 2 * CH))
    own_adj = stack(pieces(own_adj))
    lat_hi, lat_lo = pieces(latent[:, blk(1, 2)])
    grad_out = 0.5 * (folded(dot_nt(own_adj, lat_hi), 8) + dot_nt(own_adj, lat_lo)[0:8])

    fine_cot = jnp.concatenate(
        [flux_cot[:, blk(i // 2)] * inv_count[i // 2] * sea_rows[2 + i] for i in range(8)], axis=1
    )
    fine_parts = stack(pieces(fine_cot))
    small_ref[0:16, :] = folded(dot_nt(fine_parts[:, blk(2, 4)], state_b[:, blk(2, 4)]), 16)
    back_flux = dot_tn(stack([proj, proj]), fine_parts)
    own_cot = []
    for i in range(8):
        at = blk(4 + i % 2)
        if i < 2:
            out_cot = below(at)
        elif i < 4:
            out_cot = jnp.where(even, far_ref[at, :].astype(f32), near_ref[at, :].astype(f32))
        elif i < 6:
            out_cot = jnp.where(even, near_ref[at, :].astype(f32), far_ref[at, :].astype(f32))
        else:
            out_cot = above(at)
        row = (out_cot + back_flux[:, blk(i)]) * ok[(i + 2) // 4]
        put_rolled(cot_roll, i, row.astype(bf16).astype(f32), True)
        if 2 <= i < 6:
            own_cot.append(row)

    def put_slab(s, value):
        at = s * CH if s < 9 else 32 * CHUNK + (s - 9) * CH
        pay_ref[at : at + CH, :] = value.astype(bf16)

    cot_own = cot_roll[blk(1), blk(2, 4)]
    for a in range(3):
        grad = dot_nt(cot_own, act_roll[:, blk(a + 2, 4)])
        for b in range(3):
            put_slab(9 + 3 * a + b, grad[:, blk(b)])

    act_cot = dot(k2b_ref[:, 0:384], cot_roll[:, blk(2, 6)])
    act_cot += dot(k2b_ref[:, 384:768], cot_roll[:, blk(1, 6)])
    act_cot += dot(k2b_ref[:, 768:1152], cot_roll[:, blk(0, 6)])
    for i in range(6):
        row = act_cot[:, blk(i)] * slope_ref[:, blk(i)]
        put_rolled(pre_roll, i, row.astype(bf16).astype(f32), True)

    pre_own = pre_roll[blk(1), blk(1, 4)]
    for a in range(3):
        grad = dot_nt(pre_own, mixed_roll[:, blk(a + 3, 4)])
        for b in range(3):
            put_slab(3 * a + b, grad[:, blk(b)])

    in_cot = jnp.concatenate(own_cot, axis=1)
    in_cot += dot(k1b_ref[:, 0:384], pre_roll[:, blk(2, 4)])
    in_cot += dot(k1b_ref[:, 384:768], pre_roll[:, blk(1, 4)])
    in_cot += dot(k1b_ref[:, 768:1152], pre_roll[:, blk(0, 4)])
    own_surface = jnp.broadcast_to(jnp.concatenate(surface[4:8], axis=1), (8, 4 * CH))
    own_surface = stack(pieces(own_surface))
    in_hi, in_lo = pieces(in_cot)
    grad_heat = folded(dot_nt(own_surface, in_hi), 8) + dot_nt(own_surface, in_lo)[0:8]
    row_at = lax.broadcasted_iota(jnp.int32, (8, CH), 0)
    small_ref[40:48, :] = jnp.where(row_at == 0, grad_out[0:1], grad_heat[0:1])

    for k in range(16):
        at = (24 + k if k < 8 else 48 + k) * CHUNK
        if k < 3:
            pay_ref[at : at + 32, :] = two_parts(small_ref[16 * k : 16 * k + 16, :]).astype(bf16)
        else:
            pay_ref[at : at + 32, :] = jnp.zeros((32, CH), bf16)
        pay_ref[at + 32 : at + CHUNK, :] = increment.astype(bf16)


def run_step(*args):
    vmem = pl.BlockSpec(memory_space=pltpu.VMEM)
    return pl.pallas_call(
        step_kernel,
        out_shape=(
            jax.ShapeDtypeStruct((ROWS * CH, CH), bf16),
            jax.ShapeDtypeStruct((PAY, CH), bf16),
        ),
        in_specs=[vmem] * len(args),
        out_specs=(vmem, vmem),
        scratch_shapes=[
            pltpu.VMEM((3 * CH, 12 * CH), bf16),
            pltpu.VMEM((3 * CH, 10 * CH), bf16),
            pltpu.VMEM((3 * CH, 8 * CH), bf16),
            pltpu.VMEM((3 * CH, 6 * CH), bf16),
            pltpu.VMEM((CH, 6 * CH), f32),
            pltpu.VMEM((48, CH), f32),
            pltpu.VMEM((24, 4 * CH), f32),
        ],
        compiler_params=pltpu.CompilerParams(vmem_limit_bytes=32 * 1024 * 1024),
        cost_estimate=pl.CostEstimate(
            flops=1_500_000_000, bytes_accessed=4_000_000, transcendentals=300_000
        ),
    )(*args)


def hold(warm_ref, warm_adj_ref, held_ref):
    for r in range(LINES):
        held_ref[r : r + 1, :] = warm_ref[r]
        held_ref[16 + r : 17 + r, :] = warm_adj_ref[r]
    held_ref[15:16, :] = jnp.zeros((1, CH), f32)
    held_ref[31:32, :] = jnp.zeros((1, CH), f32)


def prepare_kernel(
    flag_ref, air_ref, adj_ref, sea_ref, warm_ref, warm_adj_ref, near_ref, far_ref, held_ref, rows
):
    turned = flag_ref[0] == 1
    even = lax.axis_index("core") == 0
    i = lax.broadcasted_iota(jnp.int32, (CH, CH), 0)
    j = lax.broadcasted_iota(jnp.int32, (CH, CH), 1)
    turn = jnp.where(i == jnp.where(turned, CH - 1 - j, j), 1.0, 0.0).astype(bf16)

    def canonical(ref):
        rows[...] = dot(ref[...], turn)
        stored = [rows[pl.ds(r, CH, stride=ROWS), :] for r in range(ROWS)]
        return [jnp.where(turned, stored[3 - r], stored[r]) for r in range(ROWS)]

    hold(warm_ref, warm_adj_ref, held_ref)
    start = canonical(air_ref)
    for r in range(ROWS):
        near_ref[blk(r), :] = start[r].astype(bf16)
        far_ref[blk(r), :] = start[r].astype(bf16)
    cot = canonical(adj_ref)
    for r in range(2):
        near_ref[blk(4 + r), :] = jnp.where(even, cot[2 + r], cot[r]).astype(bf16)
        far_ref[blk(4 + r), :] = jnp.where(even, cot[r], cot[2 + r]).astype(bf16)
    sea = jnp.concatenate([sea_ref[0].astype(f32), jnp.zeros((12, CH), f32)], axis=0)
    near_ref[6 * CH : HALO, :] = sea.astype(bf16)
    far_ref[6 * CH : HALO, :] = sea.astype(bf16)


def prepare(*args):
    vmem = pl.BlockSpec(memory_space=pltpu.VMEM)
    return pl.pallas_call(
        prepare_kernel,
        out_shape=(
            jax.ShapeDtypeStruct((HALO, CH), bf16),
            jax.ShapeDtypeStruct((HALO, CH), bf16),
            jax.ShapeDtypeStruct((32, CH), f32),
        ),
        in_specs=[pl.BlockSpec(memory_space=pltpu.SMEM)] + [vmem] * (len(args) - 1),
        out_specs=(vmem, vmem, vmem),
        scratch_shapes=[pltpu.VMEM((ROWS * CH, CH), f32)],
        cost_estimate=pl.CostEstimate(
            flops=20_000_000_000, bytes_accessed=700_000, transcendentals=0
        ),
    )(*args)


def choose_kernel(parcel_ref, warm_ref, warm_adj_ref, far_ref, next_ref, last_ref, out_ref, held_ref):
    zh, in_row = lax.axis_index("zh"), lax.axis_index("x") * 2 + lax.axis_index("core")
    here = jnp.where(zh == 3, 1.0, 0.0)
    hold(warm_ref, warm_adj_ref, held_ref)
    tile = lax.broadcasted_iota(jnp.int32, (TILES, 96), 0)
    lane = lax.broadcasted_iota(jnp.int32, (TILES, 96), 1)
    step, p = lane // 32, lane % 32
    wanted = (p // 8) * 32 + zh * 8 + p % 8 + step - 1
    pick = jnp.where(tile == wanted, 1.0, 0.0).astype(bf16)
    parcel = jnp.broadcast_to(parcel_ref[...], (16, TILES)).astype(f32).astype(bf16)
    line = dot(parcel, pick) - (in_row * LINES).astype(f32)
    at = lax.broadcasted_iota(jnp.int32, (16, 96), 0)
    chooser = jnp.where((at.astype(f32) == line) & (at < LINES), 1.0, 0.0).astype(bf16)
    chooser = stack([chooser] * 3)
    out_ref[...] = jnp.zeros((256, CH), f32)
    table = held_ref[...] * here + far_ref[...] + next_ref[...] + last_ref[...]
    for field in range(2):
        rows = dot_tn(chooser, stack(pieces(table[16 * field : 16 * field + 16], 3)))
        for step in range(3):
            out_ref[pl.ds(3 * field + step, 32, stride=8), :] = rows[step * 32 : step * 32 + 32]


def choose(*args):
    vmem = pl.BlockSpec(memory_space=pltpu.VMEM)
    return pl.pallas_call(
        choose_kernel,
        out_shape=jax.ShapeDtypeStruct((256, CH), f32),
        in_specs=[vmem] * len(args),
        out_specs=vmem,
        scratch_shapes=[pltpu.VMEM((32, CH), f32)],
        compiler_params=SMALL,
        cost_estimate=pl.CostEstimate(flops=20_000_000_000, bytes_accessed=200_000, transcendentals=0),
    )(*args)


def plane_sum_kernel(parcel_ref, parts_ref, out_ref):
    m0, y, zh = lax.axis_index("m0"), lax.axis_index("y"), lax.axis_index("zh")
    first = (lax.axis_index("x") * 2 + lax.axis_index("core")) * LINES
    row = lax.broadcasted_iota(jnp.int32, (16, CH), 0)
    total = jnp.zeros((CHUNK, CH), f32)
    for p in range(64):
        total += parts_ref[p * CHUNK : (p + 1) * CHUNK, :].astype(f32)
    lines = jnp.zeros((16, CH), f32)
    for p in range(32):
        tile = (p // 8) * 32 + zh * 8 + p % 8
        line = jnp.where(tile < AIR, parcel_ref[tile] - first, -1)
        at = pl.multiple_of((m0 * 32 + p) * CHUNK + 32, 16)
        increment = parts_ref[pl.ds(at, 16), :].astype(f32)
        lines += jnp.where((row == line) & (row < LINES), increment, 0.0)
    head = parts_again(total, y == 3)
    tail = jnp.where(y == 3, lines, total[32:CHUNK]).astype(bf16)
    for k in range(8):
        out_ref[k * CHUNK : k * CHUNK + 32, :] = head
        out_ref[k * CHUNK + 32 : (k + 1) * CHUNK, :] = tail


def column_sum_kernel(column_ref, sea_ref, out_ref, next_sea_ref):
    total = jnp.zeros((CHUNK, CH), f32)
    for k in range(8):
        total += column_ref[k * CHUNK : (k + 1) * CHUNK, :].astype(f32)
    total = total * norm_scale
    head = parts_again(total, lax.axis_index("y") == 3)
    tail = total[32:CHUNK].astype(bf16)
    for p in range(64):
        out_ref[p * CHUNK : p * CHUNK + 32, :] = head
        out_ref[p * CHUNK + 32 : (p + 1) * CHUNK, :] = tail
    lines = jnp.zeros((16, CH), f32)
    for zh in range(4):
        at = pl.multiple_of((zh * 2 + lax.axis_index("m1")) * CHUNK + 32, 16)
        lines += column_ref[pl.ds(at, 16), :].astype(f32)
    ocean = jnp.where(tile_place() < AIR, 0.0, 1.0)
    for r in range(LINES):
        next_sea_ref[r] = (sea_ref[r] + lines[r : r + 1]) * ocean


def finish_kernel(whole_ref, lead_ref, close_ref, entry_ref, heat_ref, coupler_ref, exit_ref):
    for s in range(9):
        lead_ref[blk(s), :] = whole_ref[blk(s), :].astype(f32)
        at = 32 * CHUNK + s * CH
        close_ref[blk(s), :] = whole_ref[at : at + CH, :].astype(f32)
    small = []
    for k in range(3):
        at = (24 + k) * CHUNK
        small.append(folded(whole_ref[at : at + 32, :].astype(f32), 16))
    small = jnp.concatenate(small, axis=0)
    coupler_ref[...] = small[0:16]
    entry_ref[...] = small[16:33]
    exit_ref[...] = small[40:41]
    heat_ref[...] = small[41:42]


def call(kernel, shapes, args, scalar=False, params=SMALL):
    vmem = pl.BlockSpec(memory_space=pltpu.VMEM)
    first = pl.BlockSpec(memory_space=pltpu.SMEM) if scalar else vmem
    return pl.pallas_call(
        kernel,
        out_shape=tuple(jax.ShapeDtypeStruct(*s) for s in shapes),
        in_specs=[first] + [vmem] * (len(args) - 1),
        out_specs=tuple(vmem for _ in shapes),
        compiler_params=params,
        cost_estimate=pl.CostEstimate(
            flops=2_000_000, bytes_accessed=1_000_000, transcendentals=0
        ),
    )(*args)


def exchange(value, axes):
    return lax.all_to_all(value, axes, 0, 0, tiled=True)


def local(
    air_fields,
    sea_warmth,
    rotation_flags,
    sea_pixel_indicator,
    panel_sea_parcel,
    opening_filter,
    closing_filter,
    warmth_injection,
    exchange_projection,
    sea_entry_matrix,
    sea_exit_matrix,
    air_adjoint_result,
    warmth_adjoint_result,
):
    sea_rows = sea_warmth.reshape(LINES, 1, CH)
    adj_rows = warmth_adjoint_result.reshape(LINES, 1, CH)
    near_pay, far_pay, held = prepare(
        rotation_flags,
        air_fields.reshape(ROWS * CH, CH),
        air_adjoint_result.reshape(ROWS * CH, CH),
        sea_pixel_indicator,
        sea_rows,
        adj_rows,
    )

    reached = [lax.ppermute(held, ("y", "zh"), [(15, at)]) for at in (14, 13, 12)]
    swap = [(i, i ^ 1) for i in range(TILES)]
    from_near = lax.ppermute(near_pay, TILE_AXES, swap)
    swap = [(i, i + 1) for i in range(1, TILES - 1, 2)]
    from_far = lax.ppermute(far_pay, TILE_AXES, swap + [(j, i) for i, j in swap])
    leaving = choose(panel_sea_parcel.reshape(1, TILES), sea_rows, adj_rows, *reached)
    warm = exchange(leaving.reshape(32, 8, CH), PLANE).reshape(256, CH)

    def stacked(weights):
        return jnp.transpose(weights, (1, 2, 0, 3)).reshape(9 * CH, CH)

    few = jnp.concatenate(
        [
            warmth_injection[None],
            sea_exit_matrix[None],
            jnp.zeros((6, CH), f32),
            sea_entry_matrix.T,
            jnp.zeros((7, CH), f32),
            exchange_projection.astype(f32),
        ]
    )
    flat = (CH, 9 * CH)
    next_rows, pay = run_step(
        warm,
        from_near,
        near_pay,
        far_pay,
        from_far,
        stacked(opening_filter),
        stacked(closing_filter),
        jnp.transpose(opening_filter, (3, 1, 2, 0)).reshape(flat),
        jnp.transpose(closing_filter, (3, 1, 2, 0)).reshape(flat),
        few,
    )

    parts = exchange(pay.reshape(64, CHUNK, CH), PAIR).reshape(PAY, CH)
    (column,) = call(
        plane_sum_kernel, [((8 * CHUNK, CH), bf16)], (panel_sea_parcel, parts), scalar=True
    )
    column = exchange(column.reshape(8, CHUNK, CH), ("zh", "m1")).reshape(8 * CHUNK, CH)
    total, next_sea = call(
        column_sum_kernel, [((PAY, CH), bf16), ((LINES, 1, CH), f32)], (column, sea_rows)
    )
    whole = exchange(total.reshape(64, CHUNK, CH), PAIR).reshape(PAY, CH)
    lead, close, entry, heat, coupler, exit_row = call(
        finish_kernel,
        [
            ((9 * CH, CH), f32),
            ((9 * CH, CH), f32),
            ((FX + 1, CH), f32),
            ((1, CH), f32),
            ((FX, CH), f32),
            ((1, CH), f32),
        ],
        (whole,),
    )

    def unstacked(rows):
        return jnp.transpose(rows.reshape(3, 3, CH, CH), (2, 0, 1, 3))

    flipped = rotation_flags[0] == 1
    next_air = jnp.transpose(next_rows.reshape(ROWS, CH, CH), (1, 0, 2))
    next_air = jnp.where(flipped, next_air[:, ::-1, ::-1], next_air)
    return (
        next_air[None, None],
        next_sea.reshape(1, 1, LINES, CH),
        unstacked(lead),
        unstacked(close),
        heat.reshape(CH),
        coupler,
        entry.T,
        exit_row.reshape(CH),
    )


def solution(mesh):
    fine = Mesh(mesh.devices.reshape(2, 2, 4, 4, 4, 2), ("m1", "m0") + TILE_AXES)
    tiles = P(("m1", "m0"), TILE_AXES)
    return jax.shard_map(
        local,
        mesh=fine,
        in_specs=(tiles, tiles, P(TILE_AXES), P(TILE_AXES))
        + (P(),) * 7
        + (tiles, tiles),
        out_specs=(tiles, tiles) + (P(),) * 6,
        check_vma=False,
    )
```

```python
import math

import jax
import jax.numpy as jnp
from jax import lax
from jax.experimental import pallas as pl
from jax.experimental.pallas import tpu as pltpu
from jax.sharding import Mesh, PartitionSpec as P

CH = 128
FX = 16
ROWS = 4
TILES = 128
AIR = 120
LINES = 15
CHUNK = 40
COLUMN = 48
HALO = 6 * CH + 16
TILE_AXES = ("y", "zh", "x", "core")
PLANE = ("y", "x", "core")
PAIR = ("m0",) + PLANE

gelu_scale = math.sqrt(2.0 / math.pi)
gelu_cubic = 0.044715
norm_scale = 1.0 / math.sqrt(4 * AIR * ROWS * CH)
EXACT = lax.Precision.HIGHEST
f32 = jnp.float32
SMALL = pltpu.CompilerParams(vmem_limit_bytes=12 * 1024 * 1024)
bf16 = jnp.bfloat16


def gelu_pair(value):
    square = value * value
    inner = gelu_scale * (value + gelu_cubic * square * value)
    tanh_val = jnp.tanh(inner)
    out = 0.5 * value * (1.0 + tanh_val)
    slope = 0.5 * (1.0 + tanh_val) + 0.5 * value * (1.0 - tanh_val * tanh_val) * gelu_scale * (
        1.0 + 3.0 * gelu_cubic * square
    )
    return (out, slope)


def dot(a, b, precision=None):
    return lax.dot_general(
        a, b, (((1,), (0,)), ((), ())), precision=precision, preferred_element_type=f32
    )


def dot_nt(a, b, precision=None):
    return lax.dot_general(
        a, b, (((1,), (1,)), ((), ())), precision=precision, preferred_element_type=f32
    )


def dot_tn(a, b):
    return lax.dot_general(a, b, (((0,), (0,)), ((), ())), preferred_element_type=f32)


def pieces(value, count=2):
    out = []
    for _ in range(count):
        out.append(value.astype(bf16))
        value = value - out[-1].astype(f32)
    return out


def stack(parts):
    return jnp.concatenate(parts, axis=0)


def folded(rows, n):
    return rows[0:n] + rows[n : 2 * n]


def blk(i, n=1):
    return slice(i * CH, (i + n) * CH)


def tile_place():
    y, zh, x, core = (lax.axis_index(a) for a in TILE_AXES)
    return ((y * 4 + zh) * 4 + x) * 2 + core


def two_parts(value):
    high = value.astype(bf16).astype(f32)
    row = lax.broadcasted_iota(jnp.int32, (8, CH), 0)
    return jnp.where(row < 4, high, value - high)


def parts_again(total):
    return two_parts(total + pltpu.roll(total, 4, 0))


def chunk_of(r):
    if r < 48 * CHUNK:
        n = r // CHUNK
        return n if n < 24 else n + 8, r % CHUNK, CHUNK - r % CHUNK
    q, at = divmod(r - 48 * CHUNK, 24)
    return 24 + q if q < 8 else 48 + q, at, 24 - at


def step_kernel(
    warm_ref,
    from_near_ref,
    near_ref,
    far_ref,
    from_far_ref,
    k1_ref,
    k2_ref,
    k1b_ref,
    k2b_ref,
    few_ref,
    next_ref,
    pay_ref,
    mixed_roll,
    act_roll,
    cot_roll,
    pre_roll,
    slope_ref,
    small_ref,
    ocean_in_ref,
    grad_ref,
):
    place = tile_place()
    mid = place < AIR
    ok = [jnp.where(t, 1.0, 0.0) for t in ((place > 0) & mid, mid, place < AIR - 1)]
    even = lax.axis_index("core") == 0
    cols = few_ref[0:8, :].T
    proj = few_ref[32:48, :].astype(bf16)
    winj, exit_col = cols[:, 0:1], cols[:, 1:2]

    def below(at):
        return jnp.where(even, from_far_ref[at, :].astype(f32), from_near_ref[at, :].astype(f32))

    def above(at):
        return jnp.where(even, from_near_ref[at, :].astype(f32), from_far_ref[at, :].astype(f32))

    def own(at):
        return near_ref[at, :].astype(f32)

    def taps(ref, a):
        return jnp.concatenate([ref[blk(3 * a + b), :] for b in range(3)], axis=1)

    def put_rolled(ref, i, value, back=False):
        ref[blk(0), blk(i)] = pltpu.roll(value, CH - 1 if back else 1, 1).astype(bf16)
        ref[blk(1), blk(i)] = value.astype(bf16)
        ref[blk(2), blk(i)] = pltpu.roll(value, 1 if back else CH - 1, 1).astype(bf16)

    sea_rows = []
    for read in (below, own, above):
        ind = read(slice(6 * CH, HALO))
        sea_rows += [ind[r : r + 1] for r in range(ROWS)]
    cell = lax.broadcasted_iota(jnp.int32, (CH, 2 * CH), 1)
    entry_at = lax.broadcasted_iota(jnp.int32, (CH, 2 * CH), 0)
    spread = (entry_at == (cell // CH) * 64 + (cell % CH) // 2).astype(bf16)
    blocks = sum(warm_ref[(24 + i) * 8 : (25 + i) * 8, :] for i in range(8))
    on_cells = dot(blocks, spread.astype(f32), EXACT)
    warm = [[on_cells[i : i + 1, blk(r)] * ok[i] for r in range(2)] for i in range(3)]
    warm_adj = [[on_cells[3 + i : 4 + i, blk(r)] * ok[i] for r in range(2)] for i in range(3)]
    surface = [warm[r // 4][(r % 4) // 2] * sea_rows[r] for r in range(12)]

    for r in range(12):
        read = (below, own, above)[r // 4]
        value = read(blk(r % 4)) * ok[r // 4] + winj * surface[r]
        put_rolled(mixed_roll, r, value.astype(bf16).astype(f32))

    pre_first = dot(taps(k1_ref, 0), mixed_roll[:, blk(0, 10)])
    pre_first += dot(taps(k1_ref, 1), mixed_roll[:, blk(1, 10)])
    pre_first += dot(taps(k1_ref, 2), mixed_roll[:, blk(2, 10)])
    for i in range(10):
        act, slope = gelu_pair(pre_first[:, blk(i)])
        m = ok[(i + 1) // 4]
        put_rolled(act_roll, i, (act * m).astype(bf16).astype(f32))
        if 2 <= i < 8:
            slope_ref[:, blk(i - 2)] = slope * m

    state = dot(taps(k2_ref, 0), act_roll[:, blk(0, 8)])
    state += dot(taps(k2_ref, 1), act_roll[:, blk(1, 8)])
    state += dot(taps(k2_ref, 2), act_roll[:, blk(2, 8)])
    state_rows = []
    for i in range(8):
        row = (state[:, blk(i)] + mixed_roll[blk(1), blk(i + 2)].astype(f32)) * ok[(i + 2) // 4]
        state_rows.append(row.astype(bf16))
    state_b = jnp.concatenate(state_rows, axis=1)
    for r in range(ROWS):
        next_ref[blk(r), :] = state_rows[2 + r]

    flux = dot(proj, state_b)
    even_lane = lax.broadcasted_iota(jnp.int32, (FX, CH), 1) % 2 == 0

    def pair_sum(v):
        return v + jnp.where(even_lane, pltpu.roll(v, CH - 1, 1), pltpu.roll(v, 1, 1))

    tile_flux, inv_count = [], []
    for q in range(4):
        sea_a, sea_b = sea_rows[2 + 2 * q], sea_rows[3 + 2 * q]
        count = pair_sum(jnp.broadcast_to(sea_a + sea_b, (FX, CH)))
        inv = 1.0 / jnp.maximum(count, 1.0)
        total = pair_sum(flux[:, blk(2 * q)] * sea_a + flux[:, blk(2 * q + 1)] * sea_b)
        tile_flux.append((total * inv).astype(bf16).astype(f32))
        inv_count.append(inv)
    block_flux = jnp.concatenate(tile_flux, axis=1)
    block_warm = jnp.concatenate([warm[0][1], warm[1][0], warm[1][1], warm[2][0]], axis=1)
    block_adj = jnp.concatenate(
        [warm_adj[0][1], warm_adj[1][0], warm_adj[1][1], warm_adj[2][0]], axis=1
    )

    ocean_in_ref[...] = jnp.zeros((24, 4 * CH), f32)
    ocean_in_ref[0:1, :] = block_warm
    ocean_in_ref[1:17, :] = block_flux
    entry_hi, entry_lo = pieces(few_ref[8:32, :])
    in_hi, in_lo = pieces(ocean_in_ref[...])
    zero = jnp.zeros((8, CH), bf16)
    pre_ocean = dot_tn(
        stack([entry_hi, entry_lo, entry_hi, zero]),
        stack([in_hi, in_hi, in_lo, jnp.zeros((8, 4 * CH), bf16)]),
    )
    latent, ocean_slope = gelu_pair(pre_ocean)
    ocean_cot = exit_col * block_adj * ocean_slope
    cot_hi, cot_lo = pieces(ocean_cot)
    entry_hi, entry_lo = pieces(few_ref[9:25, :])
    flux_cot = folded(dot(stack([entry_hi, entry_lo]), cot_hi), 16) + dot(entry_hi, cot_lo)
    increment = jnp.sum(exit_col * latent[:, blk(1, 2)], axis=0, keepdims=True)
    increment = stack(pieces(jnp.broadcast_to(increment, (16, 2 * CH))))
    increment = 0.5 * folded(dot_nt(increment, spread), 16)
    own_in = stack([in_hi, in_lo])[:, blk(1, 2)]
    grad_in = folded(dot_nt(own_in, cot_hi[:, blk(1, 2)]), 24)
    grad_in += dot_nt(in_hi[:, blk(1, 2)], cot_lo[:, blk(1, 2)])
    small_ref[16:40, :] = 0.5 * grad_in
    own_adj = jnp.broadcast_to(block_adj[:, blk(1, 2)], (8, 2 * CH))
    own_adj = stack(pieces(own_adj))
    lat_hi, lat_lo = pieces(latent[:, blk(1, 2)])
    grad_out = 0.5 * (folded(dot_nt(own_adj, lat_hi), 8) + dot_nt(own_adj, lat_lo)[0:8])

    fine_cot = jnp.concatenate(
        [flux_cot[:, blk(i // 2)] * inv_count[i // 2] * sea_rows[2 + i] for i in range(8)], axis=1
    )
    fine_parts = stack(pieces(fine_cot))
    small_ref[0:16, :] = folded(dot_nt(fine_parts[:, blk(2, 4)], state_b[:, blk(2, 4)]), 16)
    back_flux = dot_tn(stack([proj, proj]), fine_parts)
    own_cot = []
    for i in range(8):
        at = blk(4 + i % 2)
        if i < 2:
            out_cot = below(at)
        elif i < 4:
            out_cot = jnp.where(even, far_ref[at, :].astype(f32), near_ref[at, :].astype(f32))
        elif i < 6:
            out_cot = jnp.where(even, near_ref[at, :].astype(f32), far_ref[at, :].astype(f32))
        else:
            out_cot = above(at)
        row = (out_cot + back_flux[:, blk(i)]) * ok[(i + 2) // 4]
        put_rolled(cot_roll, i, row.astype(bf16).astype(f32), True)
        if 2 <= i < 6:
            own_cot.append(row)

    def put_slab(s, value):
        grad_ref[blk(s), :] = value

    cot_own = cot_roll[blk(1), blk(2, 4)]
    for a in range(3):
        grad = dot_nt(cot_own, act_roll[:, blk(a + 2, 4)])
        for b in range(3):
            put_slab(9 + 3 * a + b, grad[:, blk(b)])

    act_cot = dot(k2b_ref[:, 0:384], cot_roll[:, blk(2, 6)])
    act_cot += dot(k2b_ref[:, 384:768], cot_roll[:, blk(1, 6)])
    act_cot += dot(k2b_ref[:, 768:1152], cot_roll[:, blk(0, 6)])
    for i in range(6):
        row = act_cot[:, blk(i)] * slope_ref[:, blk(i)]
        put_rolled(pre_roll, i, row.astype(bf16).astype(f32), True)

    pre_own = pre_roll[blk(1), blk(1, 4)]
    for a in range(3):
        grad = dot_nt(pre_own, mixed_roll[:, blk(a + 3, 4)])
        for b in range(3):
            put_slab(3 * a + b, grad[:, blk(b)])

    in_cot = jnp.concatenate(own_cot, axis=1)
    in_cot += dot(k1b_ref[:, 0:384], pre_roll[:, blk(2, 4)])
    in_cot += dot(k1b_ref[:, 384:768], pre_roll[:, blk(1, 4)])
    in_cot += dot(k1b_ref[:, 768:1152], pre_roll[:, blk(0, 4)])
    own_surface = jnp.broadcast_to(jnp.concatenate(surface[4:8], axis=1), (8, 4 * CH))
    own_surface = stack(pieces(own_surface))
    in_hi, in_lo = pieces(in_cot)
    grad_heat = folded(dot_nt(own_surface, in_hi), 8) + dot_nt(own_surface, in_lo)[0:8]
    row_at = lax.broadcasted_iota(jnp.int32, (8, CH), 0)
    small_ref[40:48, :] = jnp.where(row_at == 0, grad_out[0:1], grad_heat[0:1])

    for n in range(48):
        c = n if n < 24 else n + 8
        pay_ref[c] = grad_ref[n * CHUNK : (n + 1) * CHUNK, :].astype(bf16)
    for k in range(16):
        at = 48 * CHUNK + 24 * k
        few = jnp.zeros((8, CH), f32)
        if k < 12:
            eight = small_ref[8 * (k // 2) : 8 * (k // 2) + 8, :]
            other = pltpu.roll(eight, 4, 0)
            row = lax.broadcasted_iota(jnp.int32, (8, CH), 0)
            few = two_parts(jnp.where((row < 4) == (k % 2 == 0), eight, other))
        rows = stack([grad_ref[at : at + 24, :], few, increment[0:8]])
        pay_ref[24 + k if k < 8 else 48 + k] = rows.astype(bf16)


def run_step(*args):
    vmem = pl.BlockSpec(memory_space=pltpu.VMEM)
    return pl.pallas_call(
        step_kernel,
        out_shape=(
            jax.ShapeDtypeStruct((ROWS * CH, CH), bf16),
            jax.ShapeDtypeStruct((64, CHUNK, CH), bf16),
        ),
        in_specs=[vmem] * len(args),
        out_specs=(vmem, vmem),
        scratch_shapes=[
            pltpu.VMEM((3 * CH, 12 * CH), bf16),
            pltpu.VMEM((3 * CH, 10 * CH), bf16),
            pltpu.VMEM((3 * CH, 8 * CH), bf16),
            pltpu.VMEM((3 * CH, 6 * CH), bf16),
            pltpu.VMEM((CH, 6 * CH), f32),
            pltpu.VMEM((48, CH), f32),
            pltpu.VMEM((24, 4 * CH), f32),
            pltpu.VMEM((18 * CH, CH), f32),
        ],
        compiler_params=pltpu.CompilerParams(vmem_limit_bytes=32 * 1024 * 1024),
        cost_estimate=pl.CostEstimate(
            flops=1_500_000_000, bytes_accessed=4_000_000, transcendentals=300_000
        ),
    )(*args)


def hold(warm_ref, warm_adj_ref, held_ref):
    for r in range(LINES):
        held_ref[r : r + 1, :] = warm_ref[r]
        held_ref[16 + r : 17 + r, :] = warm_adj_ref[r]
    held_ref[15:16, :] = jnp.zeros((1, CH), f32)
    held_ref[31:32, :] = jnp.zeros((1, CH), f32)


def prepare_kernel(
    flag_ref, air_ref, adj_ref, sea_ref, warm_ref, warm_adj_ref, near_ref, far_ref, held_ref, rows
):
    turned = flag_ref[0] == 1
    even = lax.axis_index("core") == 0
    i = lax.broadcasted_iota(jnp.int32, (CH, CH), 0)
    j = lax.broadcasted_iota(jnp.int32, (CH, CH), 1)
    turn = jnp.where(i == jnp.where(turned, CH - 1 - j, j), 1.0, 0.0).astype(bf16)

    def canonical(ref):
        rows[...] = dot(ref[...], turn)
        stored = [rows[pl.ds(r, CH, stride=ROWS), :] for r in range(ROWS)]
        return [jnp.where(turned, stored[3 - r], stored[r]) for r in range(ROWS)]

    hold(warm_ref, warm_adj_ref, held_ref)
    start = canonical(air_ref)
    for r in range(ROWS):
        near_ref[blk(r), :] = start[r].astype(bf16)
        far_ref[blk(r), :] = start[r].astype(bf16)
    cot = canonical(adj_ref)
    for r in range(2):
        near_ref[blk(4 + r), :] = jnp.where(even, cot[2 + r], cot[r]).astype(bf16)
        far_ref[blk(4 + r), :] = jnp.where(even, cot[r], cot[2 + r]).astype(bf16)
    sea = jnp.concatenate([sea_ref[0].astype(f32), jnp.zeros((12, CH), f32)], axis=0)
    near_ref[6 * CH : HALO, :] = sea.astype(bf16)
    far_ref[6 * CH : HALO, :] = sea.astype(bf16)


def prepare(*args):
    vmem = pl.BlockSpec(memory_space=pltpu.VMEM)
    return pl.pallas_call(
        prepare_kernel,
        out_shape=(
            jax.ShapeDtypeStruct((HALO, CH), bf16),
            jax.ShapeDtypeStruct((HALO, CH), bf16),
            jax.ShapeDtypeStruct((32, CH), f32),
        ),
        in_specs=[pl.BlockSpec(memory_space=pltpu.SMEM)] + [vmem] * (len(args) - 1),
        out_specs=(vmem, vmem, vmem),
        scratch_shapes=[pltpu.VMEM((ROWS * CH, CH), f32)],
        cost_estimate=pl.CostEstimate(
            flops=20_000_000_000, bytes_accessed=700_000, transcendentals=0
        ),
    )(*args)


def choose_kernel(parcel_ref, warm_ref, warm_adj_ref, far_ref, next_ref, last_ref, out_ref, held_ref):
    zh, in_row = lax.axis_index("zh"), lax.axis_index("x") * 2 + lax.axis_index("core")
    here = jnp.where(zh == 3, 1.0, 0.0)
    hold(warm_ref, warm_adj_ref, held_ref)
    tile = lax.broadcasted_iota(jnp.int32, (TILES, 96), 0)
    lane = lax.broadcasted_iota(jnp.int32, (TILES, 96), 1)
    step, p = lane // 32, lane % 32
    wanted = (p // 8) * 32 + zh * 8 + p % 8 + step - 1
    pick = jnp.where(tile == wanted, 1.0, 0.0).astype(bf16)
    parcel = jnp.broadcast_to(parcel_ref[...], (16, TILES)).astype(f32).astype(bf16)
    line = dot(parcel, pick) - (in_row * LINES).astype(f32)
    at = lax.broadcasted_iota(jnp.int32, (16, 96), 0)
    chooser = jnp.where((at.astype(f32) == line) & (at < LINES), 1.0, 0.0).astype(bf16)
    chooser = stack([chooser] * 3)
    out_ref[...] = jnp.zeros((256, CH), f32)
    table = held_ref[...] * here + far_ref[...] + next_ref[...] + last_ref[...]
    for field in range(2):
        rows = dot_tn(chooser, stack(pieces(table[16 * field : 16 * field + 16], 3)))
        for step in range(3):
            out_ref[pl.ds(3 * field + step, 32, stride=8), :] = rows[step * 32 : step * 32 + 32]


def choose(*args):
    vmem = pl.BlockSpec(memory_space=pltpu.VMEM)
    return pl.pallas_call(
        choose_kernel,
        out_shape=jax.ShapeDtypeStruct((256, CH), f32),
        in_specs=[vmem] * len(args),
        out_specs=vmem,
        scratch_shapes=[pltpu.VMEM((32, CH), f32)],
        compiler_params=SMALL,
        cost_estimate=pl.CostEstimate(flops=20_000_000_000, bytes_accessed=200_000, transcendentals=0),
    )(*args)


def plane_sum_kernel(parcel_ref, parts_ref, out_ref):
    m0, y, zh = lax.axis_index("m0"), lax.axis_index("y"), lax.axis_index("zh")
    first = (lax.axis_index("x") * 2 + lax.axis_index("core")) * LINES
    row = lax.broadcasted_iota(jnp.int32, (8, CH), 0)
    total = jnp.zeros((CHUNK, CH), f32)
    lines = [jnp.zeros((8, CH), f32) for _ in range(2)]
    for p in range(32):
        tile = (p // 8) * 32 + zh * 8 + p % 8
        line = jnp.where(tile < AIR, parcel_ref[tile] - first, -1)
        mine = parts_ref[m0 * 32 + p].astype(f32)
        total += mine + parts_ref[(1 - m0) * 32 + p].astype(f32)
        for h in range(2):
            wanted = (row + 8 * h == line) & (row + 8 * h < LINES)
            lines[h] += jnp.where(wanted, mine[32:40], 0.0)
    last = y == 3
    few = jnp.where(last, parts_again(total[24:32]), total[24:32])
    ends = [jnp.where(last, lines[0], total[32:40]), jnp.where(last, lines[1], 0.0)]
    column = stack([total[0:24], few] + ends).astype(bf16)
    for k in range(8):
        out_ref[k] = column


def column_sum_kernel(column_ref, sea_ref, out_ref, next_sea_ref):
    total = sum(column_ref[k].astype(f32) for k in range(8)) * norm_scale
    last = lax.axis_index("y") == 3
    few = jnp.where(last, parts_again(total[24:32]), total[24:32])
    chunk = stack([total[0:24], few, total[32:40]]).astype(bf16)
    for p in range(64):
        out_ref[p] = chunk
    m1 = lax.axis_index("m1")
    lines = sum(column_ref[zh * 2 + m1].astype(f32)[32:48] for zh in range(4))
    ocean = jnp.where(tile_place() < AIR, 0.0, 1.0)
    for r in range(LINES):
        next_sea_ref[r] = (sea_ref[r] + lines[r : r + 1]) * ocean


def finish_kernel(whole_ref, lead_ref, close_ref, entry_ref, heat_ref, coupler_ref, exit_ref):
    r = 0
    while r < 18 * CH:
        c, at, length = chunk_of(r)
        out_ref, base = (lead_ref, 0) if r < 9 * CH else (close_ref, 9 * CH)
        length = min(length, base + 9 * CH - r)
        rows = whole_ref[c].astype(f32)[at : at + length]
        out_ref[r - base : r - base + length, :] = rows
        r += length
    small = []
    for k in range(6):
        pair = []
        for c in (24 + 2 * k, 25 + 2 * k):
            few = whole_ref[c if c < 32 else c + 24].astype(f32)[24:32]
            pair.append(few + pltpu.roll(few, 4, 0))
        row = lax.broadcasted_iota(jnp.int32, (8, CH), 0)
        small.append(jnp.where(row < 4, pair[0], pair[1]))
    small = stack(small)
    coupler_ref[...] = small[0:16]
    entry_ref[...] = small[16:33]
    exit_ref[...] = small[40:41]
    heat_ref[...] = small[41:42]


def call(kernel, shapes, args, scalar=False, params=SMALL):
    vmem = pl.BlockSpec(memory_space=pltpu.VMEM)
    first = pl.BlockSpec(memory_space=pltpu.SMEM) if scalar else vmem
    return pl.pallas_call(
        kernel,
        out_shape=tuple(jax.ShapeDtypeStruct(*s) for s in shapes),
        in_specs=[first] + [vmem] * (len(args) - 1),
        out_specs=tuple(vmem for _ in shapes),
        compiler_params=params,
        cost_estimate=pl.CostEstimate(
            flops=2_000_000, bytes_accessed=1_000_000, transcendentals=0
        ),
    )(*args)


def exchange(value, axes):
    return lax.all_to_all(value, axes, 0, 0, tiled=True)


def local(
    air_fields,
    sea_warmth,
    rotation_flags,
    sea_pixel_indicator,
    panel_sea_parcel,
    opening_filter,
    closing_filter,
    warmth_injection,
    exchange_projection,
    sea_entry_matrix,
    sea_exit_matrix,
    air_adjoint_result,
    warmth_adjoint_result,
):
    sea_rows = sea_warmth.reshape(LINES, 1, CH)
    adj_rows = warmth_adjoint_result.reshape(LINES, 1, CH)
    near_pay, far_pay, held = prepare(
        rotation_flags,
        air_fields.reshape(ROWS * CH, CH),
        air_adjoint_result.reshape(ROWS * CH, CH),
        sea_pixel_indicator,
        sea_rows,
        adj_rows,
    )

    reached = [lax.ppermute(held, ("y", "zh"), [(15, at)]) for at in (14, 13, 12)]
    swap = [(i, i ^ 1) for i in range(TILES)]
    from_near = lax.ppermute(near_pay, TILE_AXES, swap)
    swap = [(i, i + 1) for i in range(1, TILES - 1, 2)]
    from_far = lax.ppermute(far_pay, TILE_AXES, swap + [(j, i) for i, j in swap])
    leaving = choose(panel_sea_parcel.reshape(1, TILES), sea_rows, adj_rows, *reached)
    warm = exchange(leaving.reshape(32, 8, CH), PLANE).reshape(256, CH)

    def stacked(weights):
        return jnp.transpose(weights, (1, 2, 0, 3)).reshape(9 * CH, CH)

    few = jnp.concatenate(
        [
            warmth_injection[None],
            sea_exit_matrix[None],
            jnp.zeros((6, CH), f32),
            sea_entry_matrix.T,
            jnp.zeros((7, CH), f32),
            exchange_projection.astype(f32),
        ]
    )
    flat = (CH, 9 * CH)
    next_rows, pay = run_step(
        warm,
        from_near,
        near_pay,
        far_pay,
        from_far,
        stacked(opening_filter),
        stacked(closing_filter),
        jnp.transpose(opening_filter, (3, 1, 2, 0)).reshape(flat),
        jnp.transpose(closing_filter, (3, 1, 2, 0)).reshape(flat),
        few,
    )

    parts = exchange(pay, PAIR)
    (column,) = call(
        plane_sum_kernel, [((8, COLUMN, CH), bf16)], (panel_sea_parcel, parts), scalar=True
    )
    column = exchange(column, ("zh", "m1"))
    total, next_sea = call(
        column_sum_kernel, [((64, CHUNK, CH), bf16), ((LINES, 1, CH), f32)], (column, sea_rows)
    )
    whole = exchange(total, PAIR)
    lead, close, entry, heat, coupler, exit_row = call(
        finish_kernel,
        [
            ((9 * CH, CH), f32),
            ((9 * CH, CH), f32),
            ((FX + 1, CH), f32),
            ((1, CH), f32),
            ((FX, CH), f32),
            ((1, CH), f32),
        ],
        (whole,),
    )

    def unstacked(rows):
        return jnp.transpose(rows.reshape(3, 3, CH, CH), (2, 0, 1, 3))

    flipped = rotation_flags[0] == 1
    next_air = jnp.transpose(next_rows.reshape(ROWS, CH, CH), (1, 0, 2))
    next_air = jnp.where(flipped, next_air[:, ::-1, ::-1], next_air)
    return (
        next_air[None, None],
        next_sea.reshape(1, 1, LINES, CH),
        unstacked(lead),
        unstacked(close),
        heat.reshape(CH),
        coupler,
        entry.T,
        exit_row.reshape(CH),
    )


def solution(mesh):
    fine = Mesh(mesh.devices.reshape(2, 2, 4, 4, 4, 2), ("m1", "m0") + TILE_AXES)
    tiles = P(("m1", "m0"), TILE_AXES)
    return jax.shard_map(
        local,
        mesh=fine,
        in_specs=(tiles, tiles, P(TILE_AXES), P(TILE_AXES))
        + (P(),) * 7
        + (tiles, tiles),
        out_specs=(tiles, tiles) + (P(),) * 6,
        check_vma=False,
    )
```

```python
import math

import jax
import jax.numpy as jnp
from jax import lax
from jax.experimental import pallas as pl
from jax.experimental.pallas import tpu as pltpu
from jax.sharding import Mesh, PartitionSpec as P

CH = 128
FX = 16
ROWS = 4
TILES = 128
AIR = 120
LINES = 15
CHUNK = 40
COLUMN = 48
HALO = 6 * CH + 16
TILE_AXES = ("y", "zh", "x", "core")
PLANE = ("y", "x", "core")
PAIR = ("m0",) + PLANE

gelu_scale = math.sqrt(2.0 / math.pi)
gelu_cubic = 0.044715
norm_scale = 1.0 / math.sqrt(4 * AIR * ROWS * CH)
EXACT = lax.Precision.HIGHEST
f32 = jnp.float32
SMALL = pltpu.CompilerParams(vmem_limit_bytes=12 * 1024 * 1024)
bf16 = jnp.bfloat16


def gelu_pair(value):
    square = value * value
    inner = gelu_scale * (value + gelu_cubic * square * value)
    tanh_val = jnp.tanh(inner)
    out = 0.5 * value * (1.0 + tanh_val)
    slope = 0.5 * (1.0 + tanh_val) + 0.5 * value * (1.0 - tanh_val * tanh_val) * gelu_scale * (
        1.0 + 3.0 * gelu_cubic * square
    )
    return (out, slope)


def dot(a, b, precision=None):
    return lax.dot_general(
        a, b, (((1,), (0,)), ((), ())), precision=precision, preferred_element_type=f32
    )


def dot_nt(a, b, precision=None):
    return lax.dot_general(
        a, b, (((1,), (1,)), ((), ())), precision=precision, preferred_element_type=f32
    )


def dot_tn(a, b):
    return lax.dot_general(a, b, (((0,), (0,)), ((), ())), preferred_element_type=f32)


def pieces(value, count=2):
    out = []
    for _ in range(count):
        out.append(value.astype(bf16))
        value = value - out[-1].astype(f32)
    return out


def stack(parts):
    return jnp.concatenate(parts, axis=0)


def folded(rows, n):
    return rows[0:n] + rows[n : 2 * n]


def blk(i, n=1):
    return slice(i * CH, (i + n) * CH)


def tile_place():
    y, zh, x, core = (lax.axis_index(a) for a in TILE_AXES)
    return ((y * 4 + zh) * 4 + x) * 2 + core


def two_parts(value):
    high = value.astype(bf16).astype(f32)
    row = lax.broadcasted_iota(jnp.int32, (8, CH), 0)
    return jnp.where(row < 4, high, value - high)


def parts_again(total):
    return two_parts(total + pltpu.roll(total, 4, 0))


def chunk_of(r):
    if r < 48 * CHUNK:
        n = r // CHUNK
        return n if n < 24 else n + 8, r % CHUNK, CHUNK - r % CHUNK
    q, at = divmod(r - 48 * CHUNK, 24)
    return 24 + q if q < 8 else 48 + q, at, 24 - at


def step_kernel(
    warm_ref,
    from_near_ref,
    near_ref,
    far_ref,
    from_far_ref,
    k1_ref,
    k2_ref,
    k1b_ref,
    k2b_ref,
    few_ref,
    next_ref,
    pay_ref,
    mixed_roll,
    act_roll,
    cot_roll,
    pre_roll,
    slope_ref,
    small_ref,
    ocean_in_ref,
    grad_ref,
):
    place = tile_place()
    mid = place < AIR
    ok = [jnp.where(t, 1.0, 0.0) for t in ((place > 0) & mid, mid, place < AIR - 1)]
    even = lax.axis_index("core") == 0
    cols = few_ref[0:8, :].T
    proj = few_ref[32:48, :].astype(bf16)
    winj, exit_col = cols[:, 0:1], cols[:, 1:2]

    def below(at):
        return jnp.where(even, from_far_ref[at, :].astype(f32), from_near_ref[at, :].astype(f32))

    def above(at):
        return jnp.where(even, from_near_ref[at, :].astype(f32), from_far_ref[at, :].astype(f32))

    def own(at):
        return near_ref[at, :].astype(f32)

    def taps(ref, a):
        return jnp.concatenate([ref[blk(3 * a + b), :] for b in range(3)], axis=1)

    def put_rolled(ref, i, value, back=False):
        ref[blk(0), blk(i)] = pltpu.roll(value, CH - 1 if back else 1, 1).astype(bf16)
        ref[blk(1), blk(i)] = value.astype(bf16)
        ref[blk(2), blk(i)] = pltpu.roll(value, 1 if back else CH - 1, 1).astype(bf16)

    sea_rows = []
    for read in (below, own, above):
        ind = read(slice(6 * CH, HALO))
        sea_rows += [ind[r : r + 1] for r in range(ROWS)]
    cell = lax.broadcasted_iota(jnp.int32, (CH, 2 * CH), 1)
    entry_at = lax.broadcasted_iota(jnp.int32, (CH, 2 * CH), 0)
    spread = (entry_at == (cell // CH) * 64 + (cell % CH) // 2).astype(bf16)
    blocks = sum(warm_ref[(24 + i) * 8 : (25 + i) * 8, :] for i in range(8))
    on_cells = dot(blocks, spread.astype(f32), EXACT)
    warm = [[on_cells[i : i + 1, blk(r)] * ok[i] for r in range(2)] for i in range(3)]
    warm_adj = [[on_cells[3 + i : 4 + i, blk(r)] * ok[i] for r in range(2)] for i in range(3)]
    surface = [warm[r // 4][(r % 4) // 2] * sea_rows[r] for r in range(12)]

    for r in range(12):
        read = (below, own, above)[r // 4]
        value = read(blk(r % 4)) * ok[r // 4] + winj * surface[r]
        put_rolled(mixed_roll, r, value.astype(bf16).astype(f32))

    pre_first = dot(taps(k1_ref, 0), mixed_roll[:, blk(0, 10)])
    pre_first += dot(taps(k1_ref, 1), mixed_roll[:, blk(1, 10)])
    pre_first += dot(taps(k1_ref, 2), mixed_roll[:, blk(2, 10)])
    for i in range(10):
        act, slope = gelu_pair(pre_first[:, blk(i)])
        m = ok[(i + 1) // 4]
        put_rolled(act_roll, i, (act * m).astype(bf16).astype(f32))
        if 2 <= i < 8:
            slope_ref[:, blk(i - 2)] = slope * m

    state = dot(taps(k2_ref, 0), act_roll[:, blk(0, 8)])
    state += dot(taps(k2_ref, 1), act_roll[:, blk(1, 8)])
    state += dot(taps(k2_ref, 2), act_roll[:, blk(2, 8)])
    state_rows = []
    for i in range(8):
        row = (state[:, blk(i)] + mixed_roll[blk(1), blk(i + 2)].astype(f32)) * ok[(i + 2) // 4]
        state_rows.append(row.astype(bf16))
    state_b = jnp.concatenate(state_rows, axis=1)
    for r in range(ROWS):
        next_ref[blk(r), :] = state_rows[2 + r]

    flux = dot(proj, state_b)
    even_lane = lax.broadcasted_iota(jnp.int32, (FX, CH), 1) % 2 == 0

    def pair_sum(v):
        return v + jnp.where(even_lane, pltpu.roll(v, CH - 1, 1), pltpu.roll(v, 1, 1))

    tile_flux, inv_count = [], []
    for q in range(4):
        sea_a, sea_b = sea_rows[2 + 2 * q], sea_rows[3 + 2 * q]
        count = pair_sum(jnp.broadcast_to(sea_a + sea_b, (FX, CH)))
        inv = 1.0 / jnp.maximum(count, 1.0)
        total = pair_sum(flux[:, blk(2 * q)] * sea_a + flux[:, blk(2 * q + 1)] * sea_b)
        tile_flux.append((total * inv).astype(bf16).astype(f32))
        inv_count.append(inv)
    block_flux = jnp.concatenate(tile_flux, axis=1)
    block_warm = jnp.concatenate([warm[0][1], warm[1][0], warm[1][1], warm[2][0]], axis=1)
    block_adj = jnp.concatenate(
        [warm_adj[0][1], warm_adj[1][0], warm_adj[1][1], warm_adj[2][0]], axis=1
    )

    ocean_in_ref[...] = jnp.zeros((24, 4 * CH), f32)
    ocean_in_ref[0:1, :] = block_warm
    ocean_in_ref[1:17, :] = block_flux
    entry_hi, entry_lo = pieces(few_ref[8:32, :])
    in_hi, in_lo = pieces(ocean_in_ref[...])
    zero = jnp.zeros((8, CH), bf16)
    pre_ocean = dot_tn(
        stack([entry_hi, entry_lo, entry_hi, zero]),
        stack([in_hi, in_hi, in_lo, jnp.zeros((8, 4 * CH), bf16)]),
    )
    latent, ocean_slope = gelu_pair(pre_ocean)
    ocean_cot = exit_col * block_adj * ocean_slope
    cot_hi, cot_lo = pieces(ocean_cot)
    entry_hi, entry_lo = pieces(few_ref[9:25, :])
    flux_cot = folded(dot(stack([entry_hi, entry_lo]), cot_hi), 16) + dot(entry_hi, cot_lo)
    increment = jnp.sum(exit_col * latent[:, blk(1, 2)], axis=0, keepdims=True)
    increment = stack(pieces(jnp.broadcast_to(increment, (16, 2 * CH))))
    increment = 0.5 * folded(dot_nt(increment, spread), 16)
    own_in = stack([in_hi, in_lo])[:, blk(1, 2)]
    grad_in = folded(dot_nt(own_in, cot_hi[:, blk(1, 2)]), 24)
    grad_in += dot_nt(in_hi[:, blk(1, 2)], cot_lo[:, blk(1, 2)])
    small_ref[16:40, :] = 0.5 * grad_in
    own_adj = jnp.broadcast_to(block_adj[:, blk(1, 2)], (8, 2 * CH))
    own_adj = stack(pieces(own_adj))
    lat_hi, lat_lo = pieces(latent[:, blk(1, 2)])
    grad_out = 0.5 * (folded(dot_nt(own_adj, lat_hi), 8) + dot_nt(own_adj, lat_lo)[0:8])

    fine_cot = jnp.concatenate(
        [flux_cot[:, blk(i // 2)] * inv_count[i // 2] * sea_rows[2 + i] for i in range(8)], axis=1
    )
    fine_parts = stack(pieces(fine_cot))
    small_ref[0:16, :] = folded(dot_nt(fine_parts[:, blk(2, 4)], state_b[:, blk(2, 4)]), 16)
    back_flux = dot_tn(stack([proj, proj]), fine_parts)
    own_cot = []
    for i in range(8):
        at = blk(4 + i % 2)
        if i < 2:
            out_cot = below(at)
        elif i < 4:
            out_cot = jnp.where(even, far_ref[at, :].astype(f32), near_ref[at, :].astype(f32))
        elif i < 6:
            out_cot = jnp.where(even, near_ref[at, :].astype(f32), far_ref[at, :].astype(f32))
        else:
            out_cot = above(at)
        row = (out_cot + back_flux[:, blk(i)]) * ok[(i + 2) // 4]
        put_rolled(cot_roll, i, row.astype(bf16).astype(f32), True)
        if 2 <= i < 6:
            own_cot.append(row)

    def put_slab(s, value):
        grad_ref[blk(s), :] = value

    cot_own = cot_roll[blk(1), blk(2, 4)]
    for a in range(3):
        grad = dot_nt(cot_own, act_roll[:, blk(a + 2, 4)])
        for b in range(3):
            put_slab(9 + 3 * a + b, grad[:, blk(b)])

    act_cot = dot(k2b_ref[:, 0:384], cot_roll[:, blk(2, 6)])
    act_cot += dot(k2b_ref[:, 384:768], cot_roll[:, blk(1, 6)])
    act_cot += dot(k2b_ref[:, 768:1152], cot_roll[:, blk(0, 6)])
    for i in range(6):
        row = act_cot[:, blk(i)] * slope_ref[:, blk(i)]
        put_rolled(pre_roll, i, row.astype(bf16).astype(f32), True)

    pre_own = pre_roll[blk(1), blk(1, 4)]
    for a in range(3):
        grad = dot_nt(pre_own, mixed_roll[:, blk(a + 3, 4)])
        for b in range(3):
            put_slab(3 * a + b, grad[:, blk(b)])

    in_cot = jnp.concatenate(own_cot, axis=1)
    in_cot += dot(k1b_ref[:, 0:384], pre_roll[:, blk(2, 4)])
    in_cot += dot(k1b_ref[:, 384:768], pre_roll[:, blk(1, 4)])
    in_cot += dot(k1b_ref[:, 768:1152], pre_roll[:, blk(0, 4)])
    own_surface = jnp.broadcast_to(jnp.concatenate(surface[4:8], axis=1), (8, 4 * CH))
    own_surface = stack(pieces(own_surface))
    in_hi, in_lo = pieces(in_cot)
    grad_heat = folded(dot_nt(own_surface, in_hi), 8) + dot_nt(own_surface, in_lo)[0:8]
    row_at = lax.broadcasted_iota(jnp.int32, (8, CH), 0)
    small_ref[40:48, :] = jnp.where(row_at == 0, grad_out[0:1], grad_heat[0:1])

    for n in range(48):
        c = n if n < 24 else n + 8
        pay_ref[c] = grad_ref[n * CHUNK : (n + 1) * CHUNK, :].astype(bf16)
    for k in range(16):
        at = 48 * CHUNK + 24 * k
        few = jnp.zeros((8, CH), f32)
        if k < 12:
            eight = small_ref[8 * (k // 2) : 8 * (k // 2) + 8, :]
            other = pltpu.roll(eight, 4, 0)
            row = lax.broadcasted_iota(jnp.int32, (8, CH), 0)
            few = two_parts(jnp.where((row < 4) == (k % 2 == 0), eight, other))
        rows = stack([grad_ref[at : at + 24, :], few, increment[0:8]])
        pay_ref[24 + k if k < 8 else 48 + k] = rows.astype(bf16)


def run_step(*args):
    vmem = pl.BlockSpec(memory_space=pltpu.VMEM)
    return pl.pallas_call(
        step_kernel,
        out_shape=(
            jax.ShapeDtypeStruct((ROWS * CH, CH), bf16),
            jax.ShapeDtypeStruct((64, CHUNK, CH), bf16),
        ),
        in_specs=[vmem] * len(args),
        out_specs=(vmem, vmem),
        scratch_shapes=[
            pltpu.VMEM((3 * CH, 12 * CH), bf16),
            pltpu.VMEM((3 * CH, 10 * CH), bf16),
            pltpu.VMEM((3 * CH, 8 * CH), bf16),
            pltpu.VMEM((3 * CH, 6 * CH), bf16),
            pltpu.VMEM((CH, 6 * CH), f32),
            pltpu.VMEM((48, CH), f32),
            pltpu.VMEM((24, 4 * CH), f32),
            pltpu.VMEM((18 * CH, CH), f32),
        ],
        compiler_params=pltpu.CompilerParams(vmem_limit_bytes=32 * 1024 * 1024),
        cost_estimate=pl.CostEstimate(
            flops=1_500_000_000, bytes_accessed=4_000_000, transcendentals=300_000
        ),
    )(*args)


def hold(warm_ref, warm_adj_ref, held_ref):
    for r in range(LINES):
        held_ref[r : r + 1, :] = warm_ref[r]
        held_ref[16 + r : 17 + r, :] = warm_adj_ref[r]
    held_ref[15:16, :] = jnp.zeros((1, CH), f32)
    held_ref[31:32, :] = jnp.zeros((1, CH), f32)


def prepare_kernel(
    flag_ref, air_ref, adj_ref, sea_ref, warm_ref, warm_adj_ref, near_ref, far_ref, held_ref, rows
):
    turned = flag_ref[0] == 1
    even = lax.axis_index("core") == 0
    i = lax.broadcasted_iota(jnp.int32, (CH, CH), 0)
    j = lax.broadcasted_iota(jnp.int32, (CH, CH), 1)
    turn = jnp.where(i == jnp.where(turned, CH - 1 - j, j), 1.0, 0.0).astype(bf16)

    def canonical(ref):
        rows[...] = dot(ref[...], turn)
        stored = [rows[pl.ds(r, CH, stride=ROWS), :] for r in range(ROWS)]
        return [jnp.where(turned, stored[3 - r], stored[r]) for r in range(ROWS)]

    hold(warm_ref, warm_adj_ref, held_ref)
    start = canonical(air_ref)
    for r in range(ROWS):
        near_ref[blk(r), :] = start[r].astype(bf16)
        far_ref[blk(r), :] = start[r].astype(bf16)
    cot = canonical(adj_ref)
    for r in range(2):
        near_ref[blk(4 + r), :] = jnp.where(even, cot[2 + r], cot[r]).astype(bf16)
        far_ref[blk(4 + r), :] = jnp.where(even, cot[r], cot[2 + r]).astype(bf16)
    sea = jnp.concatenate([sea_ref[0].astype(f32), jnp.zeros((12, CH), f32)], axis=0)
    near_ref[6 * CH : HALO, :] = sea.astype(bf16)
    far_ref[6 * CH : HALO, :] = sea.astype(bf16)


def prepare(*args):
    vmem = pl.BlockSpec(memory_space=pltpu.VMEM)
    return pl.pallas_call(
        prepare_kernel,
        out_shape=(
            jax.ShapeDtypeStruct((HALO, CH), bf16),
            jax.ShapeDtypeStruct((HALO, CH), bf16),
            jax.ShapeDtypeStruct((32, CH), f32),
        ),
        in_specs=[pl.BlockSpec(memory_space=pltpu.SMEM)] + [vmem] * (len(args) - 1),
        out_specs=(vmem, vmem, vmem),
        scratch_shapes=[pltpu.VMEM((ROWS * CH, CH), f32)],
        cost_estimate=pl.CostEstimate(
            flops=20_000_000_000, bytes_accessed=700_000, transcendentals=0
        ),
    )(*args)


def choose_kernel(parcel_ref, warm_ref, warm_adj_ref, far_ref, next_ref, last_ref, out_ref, held_ref):
    zh, in_row = lax.axis_index("zh"), lax.axis_index("x") * 2 + lax.axis_index("core")
    here = jnp.where(zh == 3, 1.0, 0.0)
    hold(warm_ref, warm_adj_ref, held_ref)
    tile = lax.broadcasted_iota(jnp.int32, (TILES, 96), 0)
    lane = lax.broadcasted_iota(jnp.int32, (TILES, 96), 1)
    step, p = lane // 32, lane % 32
    wanted = (p // 8) * 32 + zh * 8 + p % 8 + step - 1
    pick = jnp.where(tile == wanted, 1.0, 0.0).astype(bf16)
    parcel = jnp.broadcast_to(parcel_ref[...], (16, TILES)).astype(f32).astype(bf16)
    line = dot(parcel, pick) - (in_row * LINES).astype(f32)
    at = lax.broadcasted_iota(jnp.int32, (16, 96), 0)
    chooser = jnp.where((at.astype(f32) == line) & (at < LINES), 1.0, 0.0).astype(bf16)
    chooser = stack([chooser] * 3)
    out_ref[...] = jnp.zeros((256, CH), f32)
    table = held_ref[...] * here + far_ref[...] + next_ref[...] + last_ref[...]
    for field in range(2):
        rows = dot_tn(chooser, stack(pieces(table[16 * field : 16 * field + 16], 3)))
        for step in range(3):
            out_ref[pl.ds(3 * field + step, 32, stride=8), :] = rows[step * 32 : step * 32 + 32]


def choose(*args):
    vmem = pl.BlockSpec(memory_space=pltpu.VMEM)
    return pl.pallas_call(
        choose_kernel,
        out_shape=jax.ShapeDtypeStruct((256, CH), f32),
        in_specs=[vmem] * len(args),
        out_specs=vmem,
        scratch_shapes=[pltpu.VMEM((32, CH), f32)],
        compiler_params=SMALL,
        cost_estimate=pl.CostEstimate(flops=20_000_000_000, bytes_accessed=200_000, transcendentals=0),
    )(*args)


def plane_sum_kernel(parcel_ref, parts_ref, out_ref):
    m0, y, zh = lax.axis_index("m0"), lax.axis_index("y"), lax.axis_index("zh")
    first = (lax.axis_index("x") * 2 + lax.axis_index("core")) * LINES
    row = lax.broadcasted_iota(jnp.int32, (8, CH), 0)
    total = jnp.zeros((CHUNK, CH), f32)
    lines = [jnp.zeros((8, CH), f32) for _ in range(2)]
    for p in range(32):
        tile = (p // 8) * 32 + zh * 8 + p % 8
        line = jnp.where(tile < AIR, parcel_ref[tile] - first, -1)
        mine = parts_ref[m0 * 32 + p].astype(f32)
        total += mine + parts_ref[(1 - m0) * 32 + p].astype(f32)
        for h in range(2):
            wanted = (row + 8 * h == line) & (row + 8 * h < LINES)
            lines[h] += jnp.where(wanted, mine[32:40], 0.0)
    last = y == 3
    few = jnp.where(last, parts_again(total[24:32]), total[24:32])
    ends = [jnp.where(last, lines[0], total[32:40]), jnp.where(last, lines[1], 0.0)]
    column = stack([total[0:24], few] + ends).astype(bf16)
    for k in range(8):
        out_ref[k] = column


def column_sum_kernel(column_ref, sea_ref, out_ref, next_sea_ref):
    total = sum(column_ref[k].astype(f32) for k in range(8)) * norm_scale
    last = lax.axis_index("y") == 3
    few = jnp.where(last, parts_again(total[24:32]), total[24:32])
    chunk = stack([total[0:24], few, total[32:40]]).astype(bf16)
    for p in range(64):
        out_ref[p] = chunk
    m1 = lax.axis_index("m1")
    lines = sum(column_ref[m1 * 4 + zh].astype(f32)[32:48] for zh in range(4))
    ocean = jnp.where(tile_place() < AIR, 0.0, 1.0)
    for r in range(LINES):
        next_sea_ref[r] = (sea_ref[r] + lines[r : r + 1]) * ocean


def finish_kernel(whole_ref, lead_ref, close_ref, entry_ref, heat_ref, coupler_ref, exit_ref):
    r = 0
    while r < 18 * CH:
        c, at, length = chunk_of(r)
        out_ref, base = (lead_ref, 0) if r < 9 * CH else (close_ref, 9 * CH)
        length = min(length, base + 9 * CH - r)
        rows = whole_ref[c].astype(f32)[at : at + length]
        out_ref[r - base : r - base + length, :] = rows
        r += length
    small = []
    for k in range(6):
        pair = []
        for c in (24 + 2 * k, 25 + 2 * k):
            few = whole_ref[c if c < 32 else c + 24].astype(f32)[24:32]
            pair.append(few + pltpu.roll(few, 4, 0))
        row = lax.broadcasted_iota(jnp.int32, (8, CH), 0)
        small.append(jnp.where(row < 4, pair[0], pair[1]))
    small = stack(small)
    coupler_ref[...] = small[0:16]
    entry_ref[...] = small[16:33]
    exit_ref[...] = small[40:41]
    heat_ref[...] = small[41:42]


def call(kernel, shapes, args, scalar=False, params=SMALL):
    vmem = pl.BlockSpec(memory_space=pltpu.VMEM)
    first = pl.BlockSpec(memory_space=pltpu.SMEM) if scalar else vmem
    return pl.pallas_call(
        kernel,
        out_shape=tuple(jax.ShapeDtypeStruct(*s) for s in shapes),
        in_specs=[first] + [vmem] * (len(args) - 1),
        out_specs=tuple(vmem for _ in shapes),
        compiler_params=params,
        cost_estimate=pl.CostEstimate(
            flops=2_000_000, bytes_accessed=1_000_000, transcendentals=0
        ),
    )(*args)


def exchange(value, axes):
    return lax.all_to_all(value, axes, 0, 0, tiled=True)


def local(
    air_fields,
    sea_warmth,
    rotation_flags,
    sea_pixel_indicator,
    panel_sea_parcel,
    opening_filter,
    closing_filter,
    warmth_injection,
    exchange_projection,
    sea_entry_matrix,
    sea_exit_matrix,
    air_adjoint_result,
    warmth_adjoint_result,
):
    sea_rows = sea_warmth.reshape(LINES, 1, CH)
    adj_rows = warmth_adjoint_result.reshape(LINES, 1, CH)
    near_pay, far_pay, held = prepare(
        rotation_flags,
        air_fields.reshape(ROWS * CH, CH),
        air_adjoint_result.reshape(ROWS * CH, CH),
        sea_pixel_indicator,
        sea_rows,
        adj_rows,
    )

    reached = [lax.ppermute(held, ("y", "zh"), [(15, at)]) for at in (14, 13, 12)]
    swap = [(i, i ^ 1) for i in range(TILES)]
    from_near = lax.ppermute(near_pay, TILE_AXES, swap)
    swap = [(i, i + 1) for i in range(1, TILES - 1, 2)]
    from_far = lax.ppermute(far_pay, TILE_AXES, swap + [(j, i) for i, j in swap])
    leaving = choose(panel_sea_parcel.reshape(1, TILES), sea_rows, adj_rows, *reached)
    warm = exchange(leaving.reshape(32, 8, CH), PLANE).reshape(256, CH)

    def stacked(weights):
        return jnp.transpose(weights, (1, 2, 0, 3)).reshape(9 * CH, CH)

    few = jnp.concatenate(
        [
            warmth_injection[None],
            sea_exit_matrix[None],
            jnp.zeros((6, CH), f32),
            sea_entry_matrix.T,
            jnp.zeros((7, CH), f32),
            exchange_projection.astype(f32),
        ]
    )
    flat = (CH, 9 * CH)
    next_rows, pay = run_step(
        warm,
        from_near,
        near_pay,
        far_pay,
        from_far,
        stacked(opening_filter),
        stacked(closing_filter),
        jnp.transpose(opening_filter, (3, 1, 2, 0)).reshape(flat),
        jnp.transpose(closing_filter, (3, 1, 2, 0)).reshape(flat),
        few,
    )

    parts = exchange(pay, PAIR)
    (column,) = call(
        plane_sum_kernel, [((8, COLUMN, CH), bf16)], (panel_sea_parcel, parts), scalar=True
    )
    column = exchange(column, ("m1", "zh"))
    total, next_sea = call(
        column_sum_kernel, [((64, CHUNK, CH), bf16), ((LINES, 1, CH), f32)], (column, sea_rows)
    )
    whole = exchange(total, PAIR)
    lead, close, entry, heat, coupler, exit_row = call(
        finish_kernel,
        [
            ((9 * CH, CH), f32),
            ((9 * CH, CH), f32),
            ((FX + 1, CH), f32),
            ((1, CH), f32),
            ((FX, CH), f32),
            ((1, CH), f32),
        ],
        (whole,),
    )

    def unstacked(rows):
        return jnp.transpose(rows.reshape(3, 3, CH, CH), (2, 0, 1, 3))

    flipped = rotation_flags[0] == 1
    next_air = jnp.transpose(next_rows.reshape(ROWS, CH, CH), (1, 0, 2))
    next_air = jnp.where(flipped, next_air[:, ::-1, ::-1], next_air)
    return (
        next_air[None, None],
        next_sea.reshape(1, 1, LINES, CH),
        unstacked(lead),
        unstacked(close),
        heat.reshape(CH),
        coupler,
        entry.T,
        exit_row.reshape(CH),
    )


def solution(mesh):
    fine = Mesh(mesh.devices.reshape(2, 2, 4, 4, 4, 2), ("m1", "m0") + TILE_AXES)
    tiles = P(("m1", "m0"), TILE_AXES)
    return jax.shard_map(
        local,
        mesh=fine,
        in_specs=(tiles, tiles, P(TILE_AXES), P(TILE_AXES))
        + (P(),) * 7
        + (tiles, tiles),
        out_specs=(tiles, tiles) + (P(),) * 6,
        check_vma=False,
    )
```
